256 devices in a mesh: grp: 8 (over z), dom: 32 (over x, y, core).
Axes of the slice: x: 4, y: 4, z: 8, core: 2. Of those that a mesh axis runs over, the one named last changes fastest.
Arguments:
- right_side: float32 [8, 32, 5, 2048], P('grp', 'dom'), may hold values from -6 to 6
- initial_guess: float32 [8, 32, 5, 2048], P('grp', 'dom'), may hold values from -3 to 3
- fine_diag: float32 [8, 32, 5, 5, 2048], P('grp', 'dom')
- fine_inverse: float32 [8, 32, 5, 5, 2048], P('grp', 'dom')
- fine_coupling: float32 [8, 32, 6, 5, 5, 2048], P('grp', 'dom'), may hold values from -1.4 to 1.4
- fine_columns: int32 [8, 32, 6, 2048], P('grp', 'dom'), may hold values from 0 to 2303, as said below
- fine_send: int32 [8, 32, 4, 64], P('grp', 'dom'), may hold values from 0 to 2047
- fine_count: int32 [8, 32, 4], P('grp', 'dom'), may hold values from 16 to 64, as said below
- fine_aggregate: int32 [8, 32, 2048], P('grp', 'dom'), may hold values from 0 to 511, as said below
- middle_diag: float32 [8, 32, 5, 5, 512], P('grp', 'dom')
- middle_inverse: float32 [8, 32, 5, 5, 512], P('grp', 'dom')
- middle_coupling: float32 [8, 32, 6, 5, 5, 512], P('grp', 'dom'), may hold values from -1.4 to 1.4
- middle_columns: int32 [8, 32, 6, 512], P('grp', 'dom'), may hold values from 0 to 1087
- middle_aggregate: int32 [8, 32, 512], P('grp', 'dom'), may hold values from 0 to 127, as said below
- coarse_diag: float32 [8, 32, 5, 5, 128], P('grp', 'dom')
- coarse_inverse: float32 [8, 32, 5, 5, 128], P('grp', 'dom')
- coarse_coupling: float32 [8, 32, 6, 5, 5, 128], P('grp', 'dom'), may hold values from -1.4 to 1.4
- coarse_columns: int32 [8, 32, 6, 128], P('grp', 'dom'), may hold values from 0 to 511
Outputs:
- solution: float32 [8, 32, 5, 2048], P('grp', 'dom')
The draws below stay inside these ranges and needn't reach their ends.
Inputs may be any that keep to these rules, and one draw needn't show every extreme that they name: `fine_count`: at least one of the four counts of each device is 64; the others are ragged. `fine_columns`: columns below 2048 are own rows; a column 2048 + j * 64 + s names slot s of the j-th received block, with s below the sender's count. `fine_aggregate`: each middle row gathers exactly four fine rows of its device. `middle_aggregate`: each coarse row gathers exactly four middle rows of its device.
All inputs are finite; a program needn't handle non-finite values.
Results may differ from the reference program's by a relative error of at most 0.0003.
Values sent between devices are 32-bit elements; how exact they have to be, the bound alone decides.
No kernel may reach another device: no remote copies, remote signals or barrier semaphores. Data moves between devices by JAX's collectives and lax.ppermute only.
A program may use at most 128 MiB of HBM per device.

```python
import jax
import jax.numpy as jnp
from jax import lax

BLOCK = 5
NEIGHBORS = 6
ROWS_FINE = 2048
ROWS_MID = 512
ROWS_COARSE = 128
SLOT_ROWS = 64
RIM_ROWS = 32
SWEEPS_FINE = 2
SWEEPS_MID = 2
SWEEPS_COARSE = 3
GROUPS = 8
DOMAINS = 32


OFFSETS = (-2, -1, 1, 2)


coupling_scale = 0.35


def block_pair(key, level, rows):
    first = jax.random.fold_in(key, 100 + level)
    second = jax.random.fold_in(key, 200 + level)
    scales = jnp.exp(jax.random.uniform(first, (GROUPS, DOMAINS, 1, 1, rows), jnp.float32, jnp.log(1.5), jnp.log(6.0)))
    noise = 0.12 * jax.random.normal(second, (GROUPS, DOMAINS, BLOCK, BLOCK, rows), jnp.float32)
    identity = jnp.eye(BLOCK, dtype=jnp.float32)[None, None, :, :, None]
    noise = noise * (1.0 - identity)
    return (scales * (identity + noise), (identity - noise) / scales)


def coupling_blocks(key, level, rows):
    inner = jax.random.fold_in(key, 300 + level)
    shape = (GROUPS, DOMAINS, NEIGHBORS, BLOCK, BLOCK, rows)
    values = coupling_scale * jax.random.truncated_normal(inner, -4.0, 4.0, shape, jnp.float32)
    return values


def send_counts(key):
    counts = jax.random.randint(jax.random.fold_in(key, 7), (GROUPS, DOMAINS, 4), SLOT_ROWS // 4, SLOT_ROWS + 1)
    chosen = jax.random.randint(jax.random.fold_in(key, 8), (GROUPS, DOMAINS, 1), 0, 4)
    return jnp.where(jnp.arange(4)[None, None, :] == chosen, SLOT_ROWS, counts).astype(jnp.int32)


def grouped_rows(key, rows, number):
    keys = jax.random.split(key, GROUPS * DOMAINS)
    perms = jax.vmap(lambda single: jax.random.permutation(single, rows))(keys)
    return (perms % number).reshape(GROUPS, DOMAINS, rows).astype(jnp.int32)


def draw_fine_diag(key, part):
    return block_pair(key, 1, ROWS_FINE)[0]


def draw_fine_inverse(key, part):
    return block_pair(key, 1, ROWS_FINE)[1]


def draw_middle_diag(key, part):
    return block_pair(key, 2, ROWS_MID)[0]


def draw_middle_inverse(key, part):
    return block_pair(key, 2, ROWS_MID)[1]


def draw_coarse_diag(key, part):
    return block_pair(key, 3, ROWS_COARSE)[0]


def draw_coarse_inverse(key, part):
    return block_pair(key, 3, ROWS_COARSE)[1]


def draw_fine_coupling(key, part):
    return coupling_blocks(key, 1, ROWS_FINE)


def draw_middle_coupling(key, part):
    return coupling_blocks(key, 2, ROWS_MID)


def draw_coarse_coupling(key, part):
    return coupling_blocks(key, 3, ROWS_COARSE)


def draw_fine_count(key, part):
    return send_counts(key)


def draw_fine_columns(key, part):
    counts = send_counts(key)
    local_cols = jax.random.randint(jax.random.fold_in(key, 21), (GROUPS, DOMAINS, NEIGHBORS - 1, ROWS_FINE), 0, ROWS_FINE)
    received = jnp.stack([jnp.roll(counts[:, :, 3 - position], -offset, axis=1) for position, offset in enumerate(OFFSETS)], axis=-1)
    source = jax.random.randint(jax.random.fold_in(key, 22), (GROUPS, DOMAINS, 1, ROWS_FINE), 0, 4)
    limit = jnp.take_along_axis(received[:, :, None, :], source, axis=3)
    slot = jax.random.randint(jax.random.fold_in(key, 23), (GROUPS, DOMAINS, 1, ROWS_FINE), 0, limit)
    remote = ROWS_FINE + source * SLOT_ROWS + slot
    return jnp.concatenate([local_cols, remote], axis=2).astype(jnp.int32)


def draw_fine_aggregate(key, part):
    return grouped_rows(jax.random.fold_in(key, 31), ROWS_FINE, ROWS_MID)


def draw_middle_aggregate(key, part):
    return grouped_rows(jax.random.fold_in(key, 32), ROWS_MID, ROWS_COARSE)


def set_ends(drawn, rng, smallest, high):
    longest = drawn.shape.index(max(drawn.shape))
    spots = []
    for shift in (0, 1):
        where = [jax.random.randint(jax.random.fold_in(rng, axis), (), 0, length) for axis, length in enumerate(drawn.shape)]
        where[longest] = (where[longest] + shift) % drawn.shape[longest]
        spots.append(tuple(where))
    return drawn.at[spots[0]].set(smallest).at[spots[1]].set(high)


def levels(key, shape, cuts, least, top_value):
    level = 1.0
    for dim, parts in cuts:
        steps = jax.random.uniform(jax.random.fold_in(jax.random.fold_in(key, 6), dim), (parts,), jnp.float32, least / len(cuts), top_value / len(cuts))
        level = level * jnp.repeat(jnp.exp(steps), shape[dim] // parts).reshape((-1,) + (1,) * (len(shape) - 1 - dim))
    return level


def centred(key, extent, scale, most, shards=(), held_as=jnp.bfloat16):
    array = jax.random.normal(key, extent, jnp.float32) * scale
    if len(shards) > 0:
        array = levels(key, extent, shards, -0.22, 0.18) * array
    return jnp.clip(array, min=-most, max=most).astype(held_as)


def setup_inputs(seed: int = 0) -> dict:
    streams_of = jax.random.split(jax.random.key(seed), 19)
    return {
        "right_side": centred(streams_of[0], (GROUPS, DOMAINS, BLOCK, ROWS_FINE), 1.0, 6.0, ((0, 8), (1, 32)), jnp.float32),
        "initial_guess": centred(streams_of[1], (GROUPS, DOMAINS, BLOCK, ROWS_FINE), 0.5, 3.0, ((0, 8), (1, 32)), jnp.float32),
        "fine_diag": draw_fine_diag(jax.random.fold_in(streams_of[18], 71), 0),
        "fine_inverse": draw_fine_inverse(jax.random.fold_in(streams_of[18], 71), 0),
        "fine_coupling": draw_fine_coupling(jax.random.fold_in(streams_of[18], 71), 0),
        "fine_columns": draw_fine_columns(jax.random.fold_in(streams_of[18], 71), 0),
        "fine_send": set_ends(jax.random.randint(streams_of[6], (GROUPS, DOMAINS, 4, SLOT_ROWS), 0, ROWS_FINE), jax.random.fold_in(streams_of[6], 1), 0, ROWS_FINE - 1).astype(jnp.int32),
        "fine_count": draw_fine_count(jax.random.fold_in(streams_of[18], 71), 0),
        "fine_aggregate": draw_fine_aggregate(jax.random.fold_in(streams_of[18], 71), 0),
        "middle_diag": draw_middle_diag(jax.random.fold_in(streams_of[18], 71), 0),
        "middle_inverse": draw_middle_inverse(jax.random.fold_in(streams_of[18], 71), 0),
        "middle_coupling": draw_middle_coupling(jax.random.fold_in(streams_of[18], 71), 0),
        "middle_columns": set_ends(jax.random.randint(streams_of[12], (GROUPS, DOMAINS, NEIGHBORS, ROWS_MID), 0, 2 * ROWS_MID + 2 * RIM_ROWS), jax.random.fold_in(streams_of[12], 1), 0, (2 * ROWS_MID + 2 * RIM_ROWS) - 1).astype(jnp.int32),
        "middle_aggregate": draw_middle_aggregate(jax.random.fold_in(streams_of[18], 71), 0),
        "coarse_diag": draw_coarse_diag(jax.random.fold_in(streams_of[18], 71), 0),
        "coarse_inverse": draw_coarse_inverse(jax.random.fold_in(streams_of[18], 71), 0),
        "coarse_coupling": draw_coarse_coupling(jax.random.fold_in(streams_of[18], 71), 0),
        "coarse_columns": set_ends(jax.random.randint(streams_of[17], (GROUPS, DOMAINS, NEIGHBORS, ROWS_COARSE), 0, 4 * ROWS_COARSE), jax.random.fold_in(streams_of[17], 1), 0, (4 * ROWS_COARSE) - 1).astype(jnp.int32),
    }


OFFSETS = (-2, -1, 1, 2)
relaxation = 0.8


def block_product(blocks, vectors):
    return jnp.sum(blocks * vectors[..., None, :, :], axis=-2)


def apply_rows(diag, coupling, columns, field, extended):
    picked = jnp.transpose(jnp.take(extended, columns, axis=1), (1, 0, 2))
    return block_product(diag, field) + jnp.sum(block_product(coupling, picked), axis=0)


def sweep_rows(diag, inverse, coupling, columns, field, target, extended):
    image = apply_rows(diag, coupling, columns, field, extended)
    return field + relaxation * block_product(inverse, target - image)


def residual_rows(diag, coupling, columns, field, target, extended):
    return target - apply_rows(diag, coupling, columns, field, extended)


def restrict_rows(residual, aggregate, number):
    return jax.ops.segment_sum(residual.T, aggregate, num_segments=number).T


def prolong_rows(correction, aggregate):
    return jnp.take(correction, aggregate, axis=1)


def per_device(func, *arrays):
    leading = arrays[0].shape[:2]
    flat = tuple(a.reshape((-1,) + a.shape[2:]) for a in arrays)
    result = lax.map(lambda pieces: func(*pieces), flat)
    return result.reshape(leading + result.shape[1:])


def fine_extend(field, send, count):
    groups, domains, width, rows = field.shape
    slot_rows = send.shape[-1]
    spread = jnp.broadcast_to(field[:, :, None], (groups, domains, 4, width, rows))
    index = jnp.broadcast_to(send[:, :, :, None, :], (groups, domains, 4, width, slot_rows))
    live = (jnp.arange(slot_rows)[None, None, None, :] < count[:, :, :, None]).astype(jnp.float32)
    slots = jnp.take_along_axis(spread, index, axis=-1) * live[:, :, :, None, :]
    blocks = [jnp.roll(slots[:, :, 3 - position], -offset, axis=1) for position, offset in enumerate(OFFSETS)]
    return jnp.concatenate([field] + blocks, axis=-1)


def middle_extend(field):
    groups = field.shape[0]
    left = jnp.roll(field[..., -RIM_ROWS:], 1, axis=1)
    right = jnp.roll(field[..., :RIM_ROWS], -1, axis=1)
    partner = field[jnp.arange(groups) ^ 1]
    return jnp.concatenate([left, field, right, partner], axis=-1)


def coarse_extend(field):
    groups = field.shape[0]
    members = [field[jnp.arange(groups) ^ member] for member in range(4)]
    return jnp.concatenate(members, axis=-1)


def reference(right_side, initial_guess, fine_diag, fine_inverse, fine_coupling, fine_columns, fine_send, fine_count, fine_aggregate, middle_diag, middle_inverse, middle_coupling, middle_columns, middle_aggregate, coarse_diag, coarse_inverse, coarse_coupling, coarse_columns):
    def fine_sweep(field):
        extended = fine_extend(field, fine_send, fine_count)
        return per_device(sweep_rows, fine_diag, fine_inverse, fine_coupling, fine_columns, field, right_side, extended)

    def middle_sweep(field, target):
        return per_device(sweep_rows, middle_diag, middle_inverse, middle_coupling, middle_columns, field, target, middle_extend(field))

    def coarse_sweep(field, target):
        return per_device(sweep_rows, coarse_diag, coarse_inverse, coarse_coupling, coarse_columns, field, target, coarse_extend(field))

    field = initial_guess
    for step in range(SWEEPS_FINE):
        field = fine_sweep(field)
    fine_residual = per_device(residual_rows, fine_diag, fine_coupling, fine_columns, field, right_side, fine_extend(field, fine_send, fine_count))
    middle_rhs = per_device(lambda r, a: restrict_rows(r, a, ROWS_MID), fine_residual, fine_aggregate)
    middle_field = jnp.zeros_like(middle_rhs)
    for step in range(SWEEPS_MID):
        middle_field = middle_sweep(middle_field, middle_rhs)
    middle_residual = per_device(residual_rows, middle_diag, middle_coupling, middle_columns, middle_field, middle_rhs, middle_extend(middle_field))
    coarse_rhs = per_device(lambda r, a: restrict_rows(r, a, ROWS_COARSE), middle_residual, middle_aggregate)
    coarse_field = jnp.zeros_like(coarse_rhs)
    for step in range(SWEEPS_COARSE):
        coarse_field = coarse_sweep(coarse_field, coarse_rhs)
    middle_field = middle_field + per_device(prolong_rows, coarse_field, middle_aggregate)
    for step in range(SWEEPS_MID):
        middle_field = middle_sweep(middle_field, middle_rhs)
    field = field + per_device(prolong_rows, middle_field, fine_aggregate)
    for step in range(SWEEPS_FINE):
        field = fine_sweep(field)
    return field
```

```python
import functools

import jax
import jax.numpy as jnp
from jax import lax
from jax.experimental import pallas as pl
from jax.experimental.pallas import tpu as pltpu
from jax.sharding import PartitionSpec as P

ROWS_FINE = 2048
ROWS_MID = 512
ROWS_COARSE = 128
SLOT_ROWS = 64
RIM_ROWS = 32
LANES = 128
OFFSETS = (-2, -1, 1, 2)
RELAX = 0.8
F32 = jnp.float32


def lane_pick(chunk, index):
    return jnp.take_along_axis(chunk, index, axis=1, mode="promise_in_bounds")


def pick(table, index_row, chunks):
    index = jnp.broadcast_to(index_row, (8, LANES))
    low = index & (LANES - 1)
    high = index >> 7
    level = [lane_pick(table(t), low) for t in range(chunks)]
    bit = 0
    while len(level) > 1:
        odd = ((high >> bit) & 1) == 1
        level = [
            jnp.where(odd, level[i + 1], level[i]) if i + 1 < len(level) else level[i]
            for i in range(0, len(level), 2)
        ]
        bit += 1
    return level[0]


def padded(value):
    return jnp.concatenate([value, jnp.zeros((3, value.shape[1]), value.dtype)], axis=0)


def rows_of(parts):
    return jnp.concatenate([jnp.sum(part, axis=0, keepdims=True) for part in parts], axis=0)


def apply_chunk(diag, coupling, columns, table, chunks, rows, remap=None):
    own = table(None)
    parts = [diag[i, :, rows] * own for i in range(5)]
    for n in range(6):
        index = columns[n : n + 1, rows]
        if remap is not None:
            index = remap(index)
        picked = pick(table, index, chunks)[:5]
        for i in range(5):
            parts[i] = parts[i] + coupling[n, i, :, rows] * picked
    return rows_of(parts)


def inverse_chunk(inverse, value, rows):
    return rows_of([inverse[i, :, rows] * value for i in range(5)])


def lane_slice(c):
    return pl.ds(pl.multiple_of(c * LANES, LANES), LANES)


def split3(value):
    first = value.astype(jnp.bfloat16)
    rest = value - first.astype(F32)
    second = rest.astype(jnp.bfloat16)
    third = (rest - second.astype(F32)).astype(jnp.bfloat16)
    return first, second, third


def restrict(residual, aggregate, number, store):
    rows = aggregate.shape[1]
    groups = number // LANES
    total = jnp.zeros((3 * 8 * groups, LANES), F32)
    step = min(rows, 512)
    for start in range(0, rows, step):
        index = aggregate[:, start : start + step]
        value = residual(start, step)
        high = index >> 7
        low = index & (LANES - 1)
        left = []
        for piece in split3(value):
            wide = piece.astype(F32)
            left += [jnp.where(high == h, wide, 0.0) for h in range(groups)]
        left = jnp.concatenate(left, axis=0).astype(jnp.bfloat16)
        lanes = lax.broadcasted_iota(jnp.int32, (LANES, step), 0)
        hot = jnp.where(lanes == low, 1.0, 0.0).astype(jnp.bfloat16)
        total = total + lax.dot_general(
            left, hot, (((1,), (1,)), ((), ())), preferred_element_type=F32
        )
    size = 8 * groups
    summed = total[:size] + total[size : 2 * size] + total[2 * size :]
    for h in range(groups):
        store(h, summed[h * 8 : h * 8 + 8])


def load_fine(x, received, ext):
    for c in range(ROWS_FINE // LANES):
        ext[c, 0:5] = x[:, c * LANES : (c + 1) * LANES]
    for j in range(4):
        lane = (j % 2) * SLOT_ROWS
        ext[16 + j // 2, 0:5, lane : lane + SLOT_ROWS] = received[j][...]


def pack_sends(table, send, count, outs):
    position = lax.broadcasted_iota(jnp.int32, (1, SLOT_ROWS), 1)
    for pair in range(2):
        index = jnp.concatenate([send[2 * pair : 2 * pair + 1], send[2 * pair + 1 : 2 * pair + 2]], axis=1)
        picked = pick(table, index, 16)[:5]
        for half in range(2):
            j = 2 * pair + half
            live = (position < count[j]).astype(F32)
            outs[j][...] = picked[:, half * SLOT_ROWS : (half + 1) * SLOT_ROWS] * live


def send_kernel(x, send, count, s0, s1, s2, s3):
    pack_sends(
        lambda t: padded(x[:, t * LANES : (t + 1) * LANES]), send, count, (s0, s1, s2, s3)
    )


def fine_sweep_body(x, b, diag, inverse, coupling, columns, ext, result):
    def body(c, carry):
        rows = lane_slice(c)
        own = ext[c][:5]
        table = lambda t: own if t is None else ext[t]
        image = apply_chunk(diag, coupling, columns, table, 18, rows)
        change = inverse_chunk(inverse, b[:, rows] - image, rows)
        result(c, own + RELAX * change)
        return carry

    lax.fori_loop(0, 16, body, 0)


def fine_kernel(last, x, b, diag, inverse, coupling, columns, send, count, r0, r1, r2, r3, *rest):
    if last:
        new, ext = rest
        outs = None
    else:
        new, s0, s1, s2, s3, ext, fresh = rest
        outs = (s0, s1, s2, s3)
    load_fine(x, (r0, r1, r2, r3), ext)

    def result(c, value):
        new[:, lane_slice(c)] = value
        if not last:
            fresh[c, 0:5] = value

    fine_sweep_body(x, b, diag, inverse, coupling, columns, ext, result)
    if not last:
        pack_sends(lambda t: fresh[t], send, count, outs)


def down_kernel(
    x, b, diag, coupling, columns, aggregate, m_inverse, r0, r1, r2, r3, rhs, e, low_rim, high_rim, ext, residual
):
    load_fine(x, (r0, r1, r2, r3), ext)
    residual[5:8, :] = jnp.zeros((3, ROWS_FINE), F32)

    def body(c, carry):
        rows = lane_slice(c)
        own = ext[c][:5]
        table = lambda t: own if t is None else ext[t]
        image = apply_chunk(diag, coupling, columns, table, 18, rows)
        residual[0:5, rows] = b[:, rows] - image
        return carry

    lax.fori_loop(0, 16, body, 0)

    def store(h, value):
        rows = slice(h * LANES, (h + 1) * LANES)
        rhs[:, rows] = value[:5]
        e[:, rows] = RELAX * inverse_chunk(m_inverse, value[:5], rows)

    restrict(lambda s, n: residual[:, s : s + n], aggregate, ROWS_MID, store)
    send_rims(e, low_rim, high_rim)


def send_rims(e, first, last):
    first[...] = e[:, 0:RIM_ROWS]
    last[...] = e[:, ROWS_MID - RIM_ROWS : ROWS_MID]


def middle_remap(index):
    own = index - RIM_ROWS
    left = index + 2 * ROWS_MID
    right = index + ROWS_MID
    partner = index - 2 * RIM_ROWS
    return jnp.where(
        index < RIM_ROWS,
        left,
        jnp.where(
            index < RIM_ROWS + ROWS_MID,
            own,
            jnp.where(index < 2 * RIM_ROWS + ROWS_MID, right, partner),
        ),
    )


def load_middle(e, left, right, partner, ext):
    for c in range(4):
        ext[c, 0:5] = e[:, c * LANES : (c + 1) * LANES]
        ext[4 + c, 0:5] = partner[:, c * LANES : (c + 1) * LANES]
    ext[8, 0:5, 0:RIM_ROWS] = left[...]
    ext[8, 0:5, RIM_ROWS : 2 * RIM_ROWS] = right[...]


def middle_rows(e_table, c, diag, coupling, columns):
    rows = slice(c * LANES, (c + 1) * LANES)
    own = e_table[c][:5]
    table = lambda t: own if t is None else e_table[t]
    return rows, own, apply_chunk(diag, coupling, columns, table, 9, rows, middle_remap)


def middle_kernel(e, rhs, diag, inverse, coupling, columns, left, right, partner, new, first, last, ext):
    load_middle(e, left, right, partner, ext)
    for c in range(4):
        rows, own, image = middle_rows(ext, c, diag, coupling, columns)
        new[:, rows] = own + RELAX * inverse_chunk(inverse, rhs[:, rows] - image, rows)
    send_rims(new, first, last)


def coarse_down_kernel(
    e, rhs, diag, coupling, columns, left, right, partner, aggregate, c_inverse, c_rhs, c_new, ext, residual
):
    load_middle(e, left, right, partner, ext)
    residual[5:8, :] = jnp.zeros((3, ROWS_MID), F32)
    for c in range(4):
        rows, own, image = middle_rows(ext, c, diag, coupling, columns)
        residual[0:5, rows] = rhs[:, rows] - image

    def store(h, value):
        rows = slice(0, LANES)
        c_rhs[...] = value[:5]
        c_new[...] = RELAX * inverse_chunk(c_inverse, value[:5], rows)

    restrict(lambda s, n: residual[:, s : s + n], aggregate, ROWS_COARSE, store)


def coarse_rows(c_field, others, diag, inverse, coupling, columns, rhs):
    rows = slice(0, LANES)
    members = [padded(r[...]) for r in (c_field,) + others]
    own = c_field[...]
    table = lambda t: own if t is None else members[t]
    image = apply_chunk(diag, coupling, columns, table, 4, rows)
    return own + RELAX * inverse_chunk(inverse, rhs[...] - image, rows)


def coarse_kernel(field, rhs, diag, inverse, coupling, columns, p1, p2, p3, new):
    new[...] = coarse_rows(field, (p1, p2, p3), diag, inverse, coupling, columns, rhs)


def coarse_up_kernel(field, rhs, diag, inverse, coupling, columns, p1, p2, p3, e, aggregate, new, first, last):
    done = padded(coarse_rows(field, (p1, p2, p3), diag, inverse, coupling, columns, rhs))
    for c in range(4):
        rows = slice(c * LANES, (c + 1) * LANES)
        new[:, rows] = e[:, rows] + pick(lambda t: done, aggregate[:, rows], 1)[:5]
    send_rims(new, first, last)


def middle_up_kernel(
    e, rhs, diag, inverse, coupling, columns, left, right, partner, x, aggregate, send, count,
    new, s0, s1, s2, s3, ext, done, fresh
):
    load_middle(e, left, right, partner, ext)
    for c in range(4):
        rows, own, image = middle_rows(ext, c, diag, coupling, columns)
        done[c, 0:5] = own + RELAX * inverse_chunk(inverse, rhs[:, rows] - image, rows)
    for c in range(16):
        rows = slice(c * LANES, (c + 1) * LANES)
        value = x[:, rows] + pick(lambda t: done[t], aggregate[:, rows], 4)[:5]
        new[:, rows] = value
        fresh[c, 0:5] = value
    pack_sends(lambda t: fresh[t], send, count, (s0, s1, s2, s3))


VMEM = pl.BlockSpec(memory_space=pltpu.VMEM)
SMEM = pl.BlockSpec(memory_space=pltpu.SMEM)


def call(name, kernel, args, shapes, scratch=(), scalars=()):
    return pl.pallas_call(
        kernel,
        name=name,
        out_shape=[jax.ShapeDtypeStruct(s, F32) for s in shapes],
        in_specs=[SMEM if i in scalars else VMEM for i in range(len(args))],
        out_specs=[VMEM] * len(shapes),
        scratch_shapes=[pltpu.VMEM(s, F32) for s in scratch],
        compiler_params=pltpu.CompilerParams(vmem_limit_bytes=16 * 1024 * 1024),
    )(*args)


def passed_along(x, by):
    size = lax.axis_size("dom")
    return lax.ppermute(x, "dom", [(i, (i + by) % size) for i in range(size)])


def group_swap(x, mask):
    return lax.ppermute(x, "grp", [(i, i ^ mask) for i in range(lax.axis_size("grp"))])


def per_device(
    right_side, initial_guess, fine_diag, fine_inverse, fine_coupling, fine_columns, fine_send, fine_count,
    fine_aggregate, middle_diag, middle_inverse, middle_coupling, middle_columns, middle_aggregate,
    coarse_diag, coarse_inverse, coarse_coupling, coarse_columns,
):
    b, x = right_side[0, 0], initial_guess[0, 0]
    f_mats = (fine_diag[0, 0], fine_inverse[0, 0], fine_coupling[0, 0], fine_columns[0, 0])
    f_send, f_count, f_aggregate = fine_send[0, 0], fine_count[0, 0], fine_aggregate[0]
    m_mats = (middle_diag[0, 0], middle_inverse[0, 0], middle_coupling[0, 0], middle_columns[0, 0])
    m_aggregate = middle_aggregate[0]
    c_mats = (coarse_diag[0, 0], coarse_inverse[0, 0], coarse_coupling[0, 0], coarse_columns[0, 0])

    slot = (5, SLOT_ROWS)
    fine = (5, ROWS_FINE)
    mid = (5, ROWS_MID)
    coarse = (5, ROWS_COARSE)
    rim = (5, RIM_ROWS)
    f_ext, f_fresh = (18, 8, LANES), (16, 8, LANES)
    m_ext = (9, 8, LANES)

    def fine_exchange(sends):
        return [passed_along(sends[3 - j], -offset) for j, offset in enumerate(OFFSETS)]

    def middle_exchange(e, first, last):
        return [passed_along(last, 1), passed_along(first, -1), group_swap(e, 1)]

    def coarse_exchange(c):
        return [group_swap(c, mask) for mask in (1, 2, 3)]

    def fine_sweep(name, x, sends, last=False):
        received = fine_exchange(sends)
        out = call(
            name,
            functools.partial(fine_kernel, last),
            (x, b) + f_mats + (f_send, f_count, *received),
            [fine] if last else [fine] + [slot] * 4,
            [f_ext] if last else [f_ext, f_fresh],
            scalars=(7,),
        )
        return out[0], out[1:]

    sends = call("send", send_kernel, (x, f_send, f_count), [slot] * 4, scalars=(2,))
    x, sends = fine_sweep("fine_1", x, sends)
    x, sends = fine_sweep("fine_2", x, sends)
    rhs, e, first, last = call(
        "down",
        down_kernel,
        (x, b, f_mats[0], f_mats[2], f_mats[3], f_aggregate, m_mats[1], *fine_exchange(sends)),
        [mid, mid, rim, rim],
        [f_ext, (8, ROWS_FINE)],
    )

    def middle_sweep(name, e, first, last):
        return call(
            name, middle_kernel, (e, rhs) + m_mats + tuple(middle_exchange(e, first, last)),
            [mid, rim, rim], [m_ext],
        )

    e, first, last = middle_sweep("middle_2", e, first, last)
    c_rhs, c = call(
        "coarse_down",
        coarse_down_kernel,
        (e, rhs, m_mats[0], m_mats[2], m_mats[3], *middle_exchange(e, first, last), m_aggregate, c_mats[1]),
        [coarse, coarse],
        [m_ext, (8, ROWS_MID)],
    )
    (c,) = call("coarse_2", coarse_kernel, (c, c_rhs) + c_mats + tuple(coarse_exchange(c)), [coarse])
    e, first, last = call(
        "coarse_3",
        coarse_up_kernel,
        (c, c_rhs) + c_mats + tuple(coarse_exchange(c)) + (e, m_aggregate),
        [mid, rim, rim],
    )
    e, first, last = middle_sweep("middle_3", e, first, last)
    out = call(
        "middle_4",
        middle_up_kernel,
        (e, rhs) + m_mats + tuple(middle_exchange(e, first, last)) + (x, f_aggregate, f_send, f_count),
        [fine] + [slot] * 4,
        [m_ext, (4, 8, LANES), f_fresh],
        scalars=(12,),
    )
    x, sends = out[0], out[1:]
    x, sends = fine_sweep("fine_4", x, sends)
    x, _ = fine_sweep("fine_5", x, sends, last=True)
    return x[None, None]


def solution(mesh):
    def spec(rank):
        return P("grp", "dom", *([None] * (rank - 2)))

    ranks = (4, 4, 5, 5, 6, 4, 4, 3, 3, 5, 5, 6, 4, 3, 5, 5, 6, 4)
    return jax.shard_map(
        per_device,
        mesh=mesh,
        in_specs=tuple(spec(rank) for rank in ranks),
        out_specs=spec(4),
        check_vma=False,
    )
```

```python
import functools

import jax
import jax.numpy as jnp
from jax import lax
from jax.experimental import pallas as pl
from jax.experimental.pallas import tpu as pltpu
from jax.sharding import PartitionSpec as P

ROWS_FINE = 2048
ROWS_MID = 512
ROWS_COARSE = 128
SLOT_ROWS = 64
RIM_ROWS = 32
LANES = 128
OFFSETS = (-2, -1, 1, 2)
RELAX = 0.8
F32 = jnp.float32


def lane_pick(chunk, index):
    return jnp.take_along_axis(chunk, index, axis=1, mode="promise_in_bounds")


def pick(table, index_row, chunks):
    index = jnp.broadcast_to(index_row, (8, LANES))
    low = index & (LANES - 1)
    level = [lane_pick(table(t), low) for t in range(chunks)]
    bit = 0
    while len(level) > 1:
        odd = (index & (LANES << bit)) != 0
        level = [
            jnp.where(odd, level[i + 1], level[i]) if i + 1 < len(level) else level[i]
            for i in range(0, len(level), 2)
        ]
        bit += 1
    return level[0]


def padded(value):
    return jnp.concatenate([value, jnp.zeros((3, value.shape[1]), value.dtype)], axis=0)


def rows_of(parts):
    return jnp.concatenate([jnp.sum(part, axis=0, keepdims=True) for part in parts], axis=0)


def apply_chunk(diag, coupling, columns, table, chunks, rows, remap=None):
    own = table(None)
    parts = [diag[i, :, rows] * own for i in range(5)]
    for n in range(6):
        index = columns[n : n + 1, rows]
        if remap is not None:
            index = remap(index)
        picked = pick(table, index, chunks)[:5]
        for i in range(5):
            parts[i] = parts[i] + coupling[n, i, :, rows] * picked
    return rows_of(parts)


def inverse_chunk(inverse, value, rows):
    return rows_of([inverse[i, :, rows] * value for i in range(5)])


def lane_slice(c):
    return pl.ds(pl.multiple_of(c * LANES, LANES), LANES)


def split3(value):
    first = value.astype(jnp.bfloat16)
    rest = value - first.astype(F32)
    second = rest.astype(jnp.bfloat16)
    third = (rest - second.astype(F32)).astype(jnp.bfloat16)
    return first, second, third


def restrict(residual, aggregate, number, store):
    rows = aggregate.shape[1]
    groups = number // LANES
    total = jnp.zeros((3 * 8 * groups, LANES), F32)
    step = min(rows, 512)
    for start in range(0, rows, step):
        index = aggregate[:, start : start + step]
        value = residual(start, step)
        high = index >> 7
        low = index & (LANES - 1)
        left = []
        for piece in split3(value):
            wide = piece.astype(F32)
            left += [jnp.where(high == h, wide, 0.0) for h in range(groups)]
        left = jnp.concatenate(left, axis=0).astype(jnp.bfloat16)
        lanes = lax.broadcasted_iota(jnp.int32, (LANES, step), 0)
        hot = jnp.where(lanes == low, 1.0, 0.0).astype(jnp.bfloat16)
        total = total + lax.dot_general(
            left, hot, (((1,), (1,)), ((), ())), preferred_element_type=F32
        )
    size = 8 * groups
    summed = total[:size] + total[size : 2 * size] + total[2 * size :]
    for h in range(groups):
        store(h, summed[h * 8 : h * 8 + 8])


def load_fine(x, received, ext):
    for c in range(ROWS_FINE // LANES):
        ext[c, 0:5] = x[:, c * LANES : (c + 1) * LANES]
    for j in range(4):
        lane = (j % 2) * SLOT_ROWS
        ext[16 + j // 2, 0:5, lane : lane + SLOT_ROWS] = received[j][...]


def pack_sends(table, send, count, outs):
    position = lax.broadcasted_iota(jnp.int32, (1, SLOT_ROWS), 1)
    for pair in range(2):
        index = jnp.concatenate([send[2 * pair : 2 * pair + 1], send[2 * pair + 1 : 2 * pair + 2]], axis=1)
        picked = pick(table, index, 16)[:5]
        for half in range(2):
            j = 2 * pair + half
            live = (position < count[j]).astype(F32)
            outs[j][...] = picked[:, half * SLOT_ROWS : (half + 1) * SLOT_ROWS] * live


def send_kernel(x, send, count, s0, s1, s2, s3):
    pack_sends(
        lambda t: padded(x[:, t * LANES : (t + 1) * LANES]), send, count, (s0, s1, s2, s3)
    )


def fine_sweep_body(x, b, diag, inverse, coupling, columns, ext, result):
    def body(c, carry):
        rows = lane_slice(c)
        own = ext[c][:5]
        table = lambda t: own if t is None else ext[t]
        image = apply_chunk(diag, coupling, columns, table, 18, rows)
        change = inverse_chunk(inverse, b[:, rows] - image, rows)
        result(c, own + RELAX * change)
        return carry

    lax.fori_loop(0, 16, body, 0, unroll=True)


def fine_kernel(last, x, b, diag, inverse, coupling, columns, send, count, r3, r2, r1, r0, *rest):
    if last:
        new, ext = rest
        outs = None
    else:
        new, s0, s1, s2, s3, ext, fresh = rest
        outs = (s0, s1, s2, s3)
    load_fine(x, (r0, r1, r2, r3), ext)

    def result(c, value):
        new[:, lane_slice(c)] = value
        if not last:
            fresh[c, 0:5] = value

    fine_sweep_body(x, b, diag, inverse, coupling, columns, ext, result)
    if not last:
        pack_sends(lambda t: fresh[t], send, count, outs)


def down_kernel(
    x, b, diag, coupling, columns, aggregate, m_inverse, r3, r2, r1, r0, low_rim, high_rim, rhs, e, ext, residual
):
    load_fine(x, (r0, r1, r2, r3), ext)
    residual[5:8, :] = jnp.zeros((3, ROWS_FINE), F32)

    def body(c, carry):
        rows = lane_slice(c)
        own = ext[c][:5]
        table = lambda t: own if t is None else ext[t]
        image = apply_chunk(diag, coupling, columns, table, 18, rows)
        residual[0:5, rows] = b[:, rows] - image
        return carry

    lax.fori_loop(0, 16, body, 0, unroll=True)

    def store(h, value):
        rows = slice(h * LANES, (h + 1) * LANES)
        rhs[:, rows] = value[:5]
        e[:, rows] = RELAX * inverse_chunk(m_inverse, value[:5], rows)

    restrict(lambda s, n: residual[:, s : s + n], aggregate, ROWS_MID, store)
    send_rims(e, low_rim, high_rim)


def send_rims(e, first, last):
    first[...] = e[:, 0:RIM_ROWS]
    last[...] = e[:, ROWS_MID - RIM_ROWS : ROWS_MID]


def middle_remap(index):
    own = index - RIM_ROWS
    left = index + 2 * ROWS_MID
    right = index + ROWS_MID
    partner = index - 2 * RIM_ROWS
    return jnp.where(
        index < RIM_ROWS,
        left,
        jnp.where(
            index < RIM_ROWS + ROWS_MID,
            own,
            jnp.where(index < 2 * RIM_ROWS + ROWS_MID, right, partner),
        ),
    )


def load_middle(e, left, right, partner, ext):
    for c in range(4):
        ext[c, 0:5] = e[:, c * LANES : (c + 1) * LANES]
        ext[4 + c, 0:5] = partner[:, c * LANES : (c + 1) * LANES]
    ext[8, 0:5, 0:RIM_ROWS] = left[...]
    ext[8, 0:5, RIM_ROWS : 2 * RIM_ROWS] = right[...]


def middle_rows(e_table, c, diag, coupling, columns):
    rows = slice(c * LANES, (c + 1) * LANES)
    own = e_table[c][:5]
    table = lambda t: own if t is None else e_table[t]
    return rows, own, apply_chunk(diag, coupling, columns, table, 9, rows, middle_remap)


def middle_kernel(e, rhs, diag, inverse, coupling, columns, right, left, partner, first, last, new, ext):
    load_middle(e, left, right, partner, ext)
    for c in range(4):
        rows, own, image = middle_rows(ext, c, diag, coupling, columns)
        new[:, rows] = own + RELAX * inverse_chunk(inverse, rhs[:, rows] - image, rows)
    send_rims(new, first, last)


def coarse_down_kernel(
    e, rhs, diag, coupling, columns, right, left, partner, aggregate, c_inverse, c_rhs, c_new, ext, residual
):
    load_middle(e, left, right, partner, ext)
    residual[5:8, :] = jnp.zeros((3, ROWS_MID), F32)
    for c in range(4):
        rows, own, image = middle_rows(ext, c, diag, coupling, columns)
        residual[0:5, rows] = rhs[:, rows] - image

    def store(h, value):
        rows = slice(0, LANES)
        c_rhs[...] = value[:5]
        c_new[...] = RELAX * inverse_chunk(c_inverse, value[:5], rows)

    restrict(lambda s, n: residual[:, s : s + n], aggregate, ROWS_COARSE, store)


def coarse_rows(c_field, others, diag, inverse, coupling, columns, rhs):
    rows = slice(0, LANES)
    members = [padded(r[...]) for r in (c_field,) + others]
    own = c_field[...]
    table = lambda t: own if t is None else members[t]
    image = apply_chunk(diag, coupling, columns, table, 4, rows)
    return own + RELAX * inverse_chunk(inverse, rhs[...] - image, rows)


def coarse_kernel(field, rhs, diag, inverse, coupling, columns, p3, p2, p1, new):
    new[...] = coarse_rows(field, (p1, p2, p3), diag, inverse, coupling, columns, rhs)


def coarse_up_kernel(field, rhs, diag, inverse, coupling, columns, p3, p2, p1, e, aggregate, first, last, new):
    done = padded(coarse_rows(field, (p1, p2, p3), diag, inverse, coupling, columns, rhs))
    for c in range(4):
        rows = slice(c * LANES, (c + 1) * LANES)
        new[:, rows] = e[:, rows] + pick(lambda t: done, aggregate[:, rows], 1)[:5]
    send_rims(new, first, last)


def middle_up_kernel(
    e, rhs, diag, inverse, coupling, columns, right, left, partner, x, aggregate, send, count,
    new, s0, s1, s2, s3, ext, done, fresh
):
    load_middle(e, left, right, partner, ext)
    for c in range(4):
        rows, own, image = middle_rows(ext, c, diag, coupling, columns)
        done[c, 0:5] = own + RELAX * inverse_chunk(inverse, rhs[:, rows] - image, rows)
    for c in range(16):
        rows = slice(c * LANES, (c + 1) * LANES)
        value = x[:, rows] + pick(lambda t: done[t], aggregate[:, rows], 4)[:5]
        new[:, rows] = value
        fresh[c, 0:5] = value
    pack_sends(lambda t: fresh[t], send, count, (s0, s1, s2, s3))


VMEM = pl.BlockSpec(memory_space=pltpu.VMEM)
SMEM = pl.BlockSpec(memory_space=pltpu.SMEM)


def call(name, kernel, args, shapes, scratch=(), scalars=()):
    return pl.pallas_call(
        kernel,
        name=name,
        out_shape=[jax.ShapeDtypeStruct(s, F32) for s in shapes],
        in_specs=[SMEM if i in scalars else VMEM for i in range(len(args))],
        out_specs=[VMEM] * len(shapes),
        scratch_shapes=[pltpu.VMEM(s, F32) for s in scratch],
        compiler_params=pltpu.CompilerParams(vmem_limit_bytes=16 * 1024 * 1024),
    )(*args)


def passed_along(x, by):
    size = lax.axis_size("dom")
    return lax.ppermute(x, "dom", [(i, (i + by) % size) for i in range(size)])


def group_swap(x, mask):
    return lax.ppermute(x, "grp", [(i, i ^ mask) for i in range(lax.axis_size("grp"))])


def per_device(
    right_side, initial_guess, fine_diag, fine_inverse, fine_coupling, fine_columns, fine_send, fine_count,
    fine_aggregate, middle_diag, middle_inverse, middle_coupling, middle_columns, middle_aggregate,
    coarse_diag, coarse_inverse, coarse_coupling, coarse_columns,
):
    b, x = right_side[0, 0], initial_guess[0, 0]
    f_mats = (fine_diag[0, 0], fine_inverse[0, 0], fine_coupling[0, 0], fine_columns[0, 0])
    f_send, f_count, f_aggregate = fine_send[0, 0], fine_count[0, 0], fine_aggregate[0]
    m_mats = (middle_diag[0, 0], middle_inverse[0, 0], middle_coupling[0, 0], middle_columns[0, 0])
    m_aggregate = middle_aggregate[0]
    c_mats = (coarse_diag[0, 0], coarse_inverse[0, 0], coarse_coupling[0, 0], coarse_columns[0, 0])

    slot = (5, SLOT_ROWS)
    fine = (5, ROWS_FINE)
    mid = (5, ROWS_MID)
    coarse = (5, ROWS_COARSE)
    rim = (5, RIM_ROWS)
    f_ext, f_fresh = (18, 8, LANES), (16, 8, LANES)
    m_ext = (9, 8, LANES)

    def fine_exchange(sends):
        received = [passed_along(sends[3 - j], -OFFSETS[j]) for j in (3, 2, 1, 0)]
        return received

    def middle_exchange(e, first, last):
        right = passed_along(first, -1)
        left = passed_along(last, 1)
        return [right, left, group_swap(e, 1)]

    def coarse_exchange(c):
        return [group_swap(c, mask) for mask in (3, 2, 1)]

    def fine_sweep(name, x, sends, last=False):
        received = fine_exchange(sends)
        out = call(
            name,
            functools.partial(fine_kernel, last),
            (x, b) + f_mats + (f_send, f_count, *received),
            [fine] if last else [fine] + [slot] * 4,
            [f_ext] if last else [f_ext, f_fresh],
            scalars=(7,),
        )
        return out[0], out[1:]

    sends = call("send", send_kernel, (x, f_send, f_count), [slot] * 4, scalars=(2,))
    x, sends = fine_sweep("fine_1", x, sends)
    x, sends = fine_sweep("fine_2", x, sends)
    first, last, rhs, e = call(
        "down",
        down_kernel,
        (x, b, f_mats[0], f_mats[2], f_mats[3], f_aggregate, m_mats[1], *fine_exchange(sends)),
        [rim, rim, mid, mid],
        [f_ext, (8, ROWS_FINE)],
    )

    def middle_sweep(name, e, first, last):
        return call(
            name, middle_kernel, (e, rhs) + m_mats + tuple(middle_exchange(e, first, last)),
            [rim, rim, mid], [m_ext],
        )

    first, last, e = middle_sweep("middle_2", e, first, last)
    c_rhs, c = call(
        "coarse_down",
        coarse_down_kernel,
        (e, rhs, m_mats[0], m_mats[2], m_mats[3], *middle_exchange(e, first, last), m_aggregate, c_mats[1]),
        [coarse, coarse],
        [m_ext, (8, ROWS_MID)],
    )
    (c,) = call("coarse_2", coarse_kernel, (c, c_rhs) + c_mats + tuple(coarse_exchange(c)), [coarse])
    first, last, e = call(
        "coarse_3",
        coarse_up_kernel,
        (c, c_rhs) + c_mats + tuple(coarse_exchange(c)) + (e, m_aggregate),
        [rim, rim, mid],
    )
    first, last, e = middle_sweep("middle_3", e, first, last)
    out = call(
        "middle_4",
        middle_up_kernel,
        (e, rhs) + m_mats + tuple(middle_exchange(e, first, last)) + (x, f_aggregate, f_send, f_count),
        [fine] + [slot] * 4,
        [m_ext, (4, 8, LANES), f_fresh],
        scalars=(12,),
    )
    x, sends = out[0], out[1:]
    x, sends = fine_sweep("fine_4", x, sends)
    x, _ = fine_sweep("fine_5", x, sends, last=True)
    return x[None, None]


def solution(mesh):
    def spec(rank):
        return P("grp", "dom", *([None] * (rank - 2)))

    ranks = (4, 4, 5, 5, 6, 4, 4, 3, 3, 5, 5, 6, 4, 3, 5, 5, 6, 4)
    return jax.shard_map(
        per_device,
        mesh=mesh,
        in_specs=tuple(spec(rank) for rank in ranks),
        out_specs=spec(4),
        check_vma=False,
    )
```

```python
import functools

import jax
import jax.numpy as jnp
from jax import lax
from jax.experimental import pallas as pl
from jax.experimental.pallas import tpu as pltpu
from jax.sharding import PartitionSpec as P

ROWS_FINE = 2048
ROWS_MID = 512
ROWS_COARSE = 128
SLOT_ROWS = 64
RIM_ROWS = 32
LANES = 128
OFFSETS = (-2, -1, 1, 2)
RELAX = 0.8
F32 = jnp.float32


def lane_pick(chunk, index):
    return jnp.take_along_axis(chunk, index, axis=1, mode="promise_in_bounds")


def pick(table, index_row, chunks):
    index = jnp.broadcast_to(index_row, (8, LANES))
    low = index & (LANES - 1)
    level = [lane_pick(table(t), low) for t in range(chunks)]
    bit = 0
    while len(level) > 1:
        odd = (index & (LANES << bit)) != 0
        level = [
            jnp.where(odd, level[i + 1], level[i]) if i + 1 < len(level) else level[i]
            for i in range(0, len(level), 2)
        ]
        bit += 1
    return level[0]


def padded(value):
    return jnp.concatenate([value, jnp.zeros((3, value.shape[1]), value.dtype)], axis=0)


def rows_of(parts):
    return jnp.concatenate([jnp.sum(part, axis=0, keepdims=True) for part in parts], axis=0)


def apply_chunk(diag, coupling, columns, table, chunks, rows, remap=None):
    own = table(None)
    parts = [diag[i, :, rows] * own for i in range(5)]
    for n in range(6):
        index = columns[n : n + 1, rows]
        if remap is not None:
            index = remap(index)
        picked = pick(table, index, chunks)[:5]
        for i in range(5):
            parts[i] = parts[i] + coupling[n, i, :, rows] * picked
    return rows_of(parts)


def inverse_chunk(inverse, value, rows):
    return rows_of([inverse[i, :, rows] * value for i in range(5)])


def lane_slice(c):
    return pl.ds(pl.multiple_of(c * LANES, LANES), LANES)


def split3(value):
    first = value.astype(jnp.bfloat16)
    rest = value - first.astype(F32)
    second = rest.astype(jnp.bfloat16)
    third = (rest - second.astype(F32)).astype(jnp.bfloat16)
    return first, second, third


def restrict(residual, aggregate, number, store):
    rows = aggregate.shape[1]
    groups = number // LANES
    total = jnp.zeros((3 * 8 * groups, LANES), F32)
    step = min(rows, 512)
    for start in range(0, rows, step):
        index = aggregate[:, start : start + step]
        value = residual(start, step)
        high = index >> 7
        low = index & (LANES - 1)
        left = []
        for piece in split3(value):
            wide = piece.astype(F32)
            left += [jnp.where(high == h, wide, 0.0) for h in range(groups)]
        left = jnp.concatenate(left, axis=0).astype(jnp.bfloat16)
        lanes = lax.broadcasted_iota(jnp.int32, (LANES, step), 0)
        hot = jnp.where(lanes == low, 1.0, 0.0).astype(jnp.bfloat16)
        total = total + lax.dot_general(
            left, hot, (((1,), (1,)), ((), ())), preferred_element_type=F32
        )
    size = 8 * groups
    summed = total[:size] + total[size : 2 * size] + total[2 * size :]
    for h in range(groups):
        store(h, summed[h * 8 : h * 8 + 8])


def load_fine(x, received, ext):
    for c in range(ROWS_FINE // LANES):
        ext[c, 0:5] = x[:, c * LANES : (c + 1) * LANES]
    for j in range(4):
        lane = (j % 2) * SLOT_ROWS
        ext[16 + j // 2, 0:5, lane : lane + SLOT_ROWS] = received[j][...]


def pack_sends(table, send, count, outs):
    position = lax.broadcasted_iota(jnp.int32, (1, SLOT_ROWS), 1)
    for pair in range(2):
        index = jnp.concatenate([send[2 * pair : 2 * pair + 1], send[2 * pair + 1 : 2 * pair + 2]], axis=1)
        picked = pick(table, index, 16)[:5]
        for half in range(2):
            j = 2 * pair + half
            live = (position < count[j]).astype(F32)
            outs[j][...] = picked[:, half * SLOT_ROWS : (half + 1) * SLOT_ROWS] * live


def send_kernel(x, send, count, s0, s1, s2, s3):
    pack_sends(
        lambda t: padded(x[:, t * LANES : (t + 1) * LANES]), send, count, (s0, s1, s2, s3)
    )


def fine_sweep_body(x, b, diag, inverse, coupling, columns, ext, result):
    def body(c, carry):
        rows = lane_slice(c)
        own = ext[c][:5]
        table = lambda t: own if t is None else ext[t]
        image = apply_chunk(diag, coupling, columns, table, 18, rows)
        change = inverse_chunk(inverse, b[:, rows] - image, rows)
        result(c, own + RELAX * change)
        return carry

    lax.fori_loop(0, 16, body, 0, unroll=4)


def fine_kernel(last, x, b, diag, inverse, coupling, columns, send, count, r3, r2, r1, r0, *rest):
    if last:
        new, ext = rest
        outs = None
    else:
        new, s0, s1, s2, s3, ext, fresh = rest
        outs = (s0, s1, s2, s3)
    load_fine(x, (r0, r1, r2, r3), ext)

    def result(c, value):
        new[:, lane_slice(c)] = value
        if not last:
            fresh[c, 0:5] = value

    fine_sweep_body(x, b, diag, inverse, coupling, columns, ext, result)
    if not last:
        pack_sends(lambda t: fresh[t], send, count, outs)


def down_kernel(
    x, b, diag, coupling, columns, aggregate, m_inverse, r3, r2, r1, r0, rhs, e, ext, residual
):
    load_fine(x, (r0, r1, r2, r3), ext)
    residual[5:8, :] = jnp.zeros((3, ROWS_FINE), F32)

    def body(c, carry):
        rows = lane_slice(c)
        own = ext[c][:5]
        table = lambda t: own if t is None else ext[t]
        image = apply_chunk(diag, coupling, columns, table, 18, rows)
        residual[0:5, rows] = b[:, rows] - image
        return carry

    lax.fori_loop(0, 16, body, 0, unroll=4)

    def store(h, value):
        rows = slice(h * LANES, (h + 1) * LANES)
        rhs[:, rows] = value[:5]
        e[:, rows] = RELAX * inverse_chunk(m_inverse, value[:5], rows)

    restrict(lambda s, n: residual[:, s : s + n], aggregate, ROWS_MID, store)


def middle_remap(index):
    own = index - RIM_ROWS
    left = index + 2 * ROWS_MID
    right = index + ROWS_MID
    partner = index - 2 * RIM_ROWS
    return jnp.where(
        index < RIM_ROWS,
        left,
        jnp.where(
            index < RIM_ROWS + ROWS_MID,
            own,
            jnp.where(index < 2 * RIM_ROWS + ROWS_MID, right, partner),
        ),
    )


def load_middle(e, left, right, partner, ext):
    for c in range(4):
        ext[c, 0:5] = e[:, c * LANES : (c + 1) * LANES]
        ext[4 + c, 0:5] = partner[:, c * LANES : (c + 1) * LANES]
    ext[8, 0:5, 0:RIM_ROWS] = left[:, ROWS_MID - RIM_ROWS : ROWS_MID]
    ext[8, 0:5, RIM_ROWS : 2 * RIM_ROWS] = right[:, 0:RIM_ROWS]


def middle_rows(e_table, c, diag, coupling, columns):
    rows = slice(c * LANES, (c + 1) * LANES)
    own = e_table[c][:5]
    table = lambda t: own if t is None else e_table[t]
    return rows, own, apply_chunk(diag, coupling, columns, table, 9, rows, middle_remap)


def middle_kernel(e, rhs, diag, inverse, coupling, columns, right, left, partner, new, ext):
    load_middle(e, left, right, partner, ext)
    for c in range(4):
        rows, own, image = middle_rows(ext, c, diag, coupling, columns)
        new[:, rows] = own + RELAX * inverse_chunk(inverse, rhs[:, rows] - image, rows)


def coarse_down_kernel(
    e, rhs, diag, coupling, columns, right, left, partner, aggregate, c_inverse, c_rhs, c_new, ext, residual
):
    load_middle(e, left, right, partner, ext)
    residual[5:8, :] = jnp.zeros((3, ROWS_MID), F32)
    for c in range(4):
        rows, own, image = middle_rows(ext, c, diag, coupling, columns)
        residual[0:5, rows] = rhs[:, rows] - image

    def store(h, value):
        rows = slice(0, LANES)
        c_rhs[...] = value[:5]
        c_new[...] = RELAX * inverse_chunk(c_inverse, value[:5], rows)

    restrict(lambda s, n: residual[:, s : s + n], aggregate, ROWS_COARSE, store)


def coarse_rows(c_field, others, diag, inverse, coupling, columns, rhs):
    rows = slice(0, LANES)
    members = [padded(r[...]) for r in (c_field,) + others]
    own = c_field[...]
    table = lambda t: own if t is None else members[t]
    image = apply_chunk(diag, coupling, columns, table, 4, rows)
    return own + RELAX * inverse_chunk(inverse, rhs[...] - image, rows)


def coarse_kernel(field, rhs, diag, inverse, coupling, columns, p3, p2, p1, new):
    new[...] = coarse_rows(field, (p1, p2, p3), diag, inverse, coupling, columns, rhs)


def coarse_up_kernel(field, rhs, diag, inverse, coupling, columns, p3, p2, p1, e, aggregate, new):
    done = padded(coarse_rows(field, (p1, p2, p3), diag, inverse, coupling, columns, rhs))
    for c in range(4):
        rows = slice(c * LANES, (c + 1) * LANES)
        new[:, rows] = e[:, rows] + pick(lambda t: done, aggregate[:, rows], 1)[:5]


def middle_up_kernel(
    e, rhs, diag, inverse, coupling, columns, right, left, partner, x, aggregate, send, count,
    new, s0, s1, s2, s3, ext, done, fresh
):
    load_middle(e, left, right, partner, ext)
    for c in range(4):
        rows, own, image = middle_rows(ext, c, diag, coupling, columns)
        done[c, 0:5] = own + RELAX * inverse_chunk(inverse, rhs[:, rows] - image, rows)
    for c in range(16):
        rows = slice(c * LANES, (c + 1) * LANES)
        value = x[:, rows] + pick(lambda t: done[t], aggregate[:, rows], 4)[:5]
        new[:, rows] = value
        fresh[c, 0:5] = value
    pack_sends(lambda t: fresh[t], send, count, (s0, s1, s2, s3))


VMEM = pl.BlockSpec(memory_space=pltpu.VMEM)
SMEM = pl.BlockSpec(memory_space=pltpu.SMEM)


def call(name, kernel, args, shapes, scratch=(), scalars=()):
    return pl.pallas_call(
        kernel,
        name=name,
        out_shape=[jax.ShapeDtypeStruct(s, F32) for s in shapes],
        in_specs=[SMEM if i in scalars else VMEM for i in range(len(args))],
        out_specs=[VMEM] * len(shapes),
        scratch_shapes=[pltpu.VMEM(s, F32) for s in scratch],
        compiler_params=pltpu.CompilerParams(vmem_limit_bytes=16 * 1024 * 1024),
    )(*args)


def passed_along(x, by):
    size = lax.axis_size("dom")
    return lax.ppermute(x, "dom", [(i, (i + by) % size) for i in range(size)])


def group_swap(x, mask):
    return lax.ppermute(x, "grp", [(i, i ^ mask) for i in range(lax.axis_size("grp"))])


def per_device(
    right_side, initial_guess, fine_diag, fine_inverse, fine_coupling, fine_columns, fine_send, fine_count,
    fine_aggregate, middle_diag, middle_inverse, middle_coupling, middle_columns, middle_aggregate,
    coarse_diag, coarse_inverse, coarse_coupling, coarse_columns,
):
    b, x = right_side[0, 0], initial_guess[0, 0]
    f_mats = (fine_diag[0, 0], fine_inverse[0, 0], fine_coupling[0, 0], fine_columns[0, 0])
    f_send, f_count, f_aggregate = fine_send[0, 0], fine_count[0, 0], fine_aggregate[0]
    m_mats = (middle_diag[0, 0], middle_inverse[0, 0], middle_coupling[0, 0], middle_columns[0, 0])
    m_aggregate = middle_aggregate[0]
    c_mats = (coarse_diag[0, 0], coarse_inverse[0, 0], coarse_coupling[0, 0], coarse_columns[0, 0])

    slot = (5, SLOT_ROWS)
    fine = (5, ROWS_FINE)
    mid = (5, ROWS_MID)
    coarse = (5, ROWS_COARSE)
    f_ext, f_fresh = (18, 8, LANES), (16, 8, LANES)
    m_ext = (9, 8, LANES)

    def fine_exchange(sends):
        received = [passed_along(sends[3 - j], -OFFSETS[j]) for j in (3, 2, 1, 0)]
        return received

    def middle_exchange(e):
        right = passed_along(e, -1)
        left = passed_along(e, 1)
        return [right, left, group_swap(e, 1)]

    def coarse_exchange(c):
        return [group_swap(c, mask) for mask in (3, 2, 1)]

    def fine_sweep(name, x, sends, last=False):
        received = fine_exchange(sends)
        out = call(
            name,
            functools.partial(fine_kernel, last),
            (x, b) + f_mats + (f_send, f_count, *received),
            [fine] if last else [fine] + [slot] * 4,
            [f_ext] if last else [f_ext, f_fresh],
            scalars=(7,),
        )
        return out[0], out[1:]

    sends = call("send", send_kernel, (x, f_send, f_count), [slot] * 4, scalars=(2,))
    x, sends = fine_sweep("fine_1", x, sends)
    x, sends = fine_sweep("fine_2", x, sends)
    rhs, e = call(
        "down",
        down_kernel,
        (x, b, f_mats[0], f_mats[2], f_mats[3], f_aggregate, m_mats[1], *fine_exchange(sends)),
        [mid, mid],
        [f_ext, (8, ROWS_FINE)],
    )

    def middle_sweep(name, e):
        return call(
            name, middle_kernel, (e, rhs) + m_mats + tuple(middle_exchange(e)),
            [mid], [m_ext],
        )

    (e,) = middle_sweep("middle_2", e)
    c_rhs, c = call(
        "coarse_down",
        coarse_down_kernel,
        (e, rhs, m_mats[0], m_mats[2], m_mats[3], *middle_exchange(e), m_aggregate, c_mats[1]),
        [coarse, coarse],
        [m_ext, (8, ROWS_MID)],
    )
    (c,) = call("coarse_2", coarse_kernel, (c, c_rhs) + c_mats + tuple(coarse_exchange(c)), [coarse])
    (e,) = call(
        "coarse_3",
        coarse_up_kernel,
        (c, c_rhs) + c_mats + tuple(coarse_exchange(c)) + (e, m_aggregate),
        [mid],
    )
    (e,) = middle_sweep("middle_3", e)
    out = call(
        "middle_4",
        middle_up_kernel,
        (e, rhs) + m_mats + tuple(middle_exchange(e)) + (x, f_aggregate, f_send, f_count),
        [fine] + [slot] * 4,
        [m_ext, (4, 8, LANES), f_fresh],
        scalars=(12,),
    )
    x, sends = out[0], out[1:]
    x, sends = fine_sweep("fine_4", x, sends)
    x, _ = fine_sweep("fine_5", x, sends, last=True)
    return x[None, None]


def solution(mesh):
    def spec(rank):
        return P("grp", "dom", *([None] * (rank - 2)))

    ranks = (4, 4, 5, 5, 6, 4, 4, 3, 3, 5, 5, 6, 4, 3, 5, 5, 6, 4)
    return jax.shard_map(
        per_device,
        mesh=mesh,
        in_specs=tuple(spec(rank) for rank in ranks),
        out_specs=spec(4),
        check_vma=False,
    )
```

```python
import functools

import jax
import jax.numpy as jnp
from jax import lax
from jax.experimental import pallas as pl
from jax.experimental.pallas import tpu as pltpu
from jax.sharding import PartitionSpec as P

ROWS_FINE = 2048
ROWS_MID = 512
ROWS_COARSE = 128
SLOT_ROWS = 64
RIM_ROWS = 32
LANES = 128
OFFSETS = (-2, -1, 1, 2)
RELAX = 0.8
F32 = jnp.float32


def lane_pick(chunk, index):
    return jnp.take_along_axis(chunk, index, axis=1, mode="promise_in_bounds")


def decode(index, chunks):
    low = index & (LANES - 1)
    odd = [(index & (LANES << bit)) != 0 for bit in range((chunks - 1).bit_length())]
    return low, odd


def pick(table, decoded, chunks):
    low, odd = decoded
    level = [lane_pick(jnp.broadcast_to(table(t), low.shape), low) for t in range(chunks)]
    for bit in odd:
        level = [
            jnp.where(bit, level[i + 1], level[i]) if i + 1 < len(level) else level[i]
            for i in range(0, len(level), 2)
        ]
    return level[0]


def product(total, blocks, vectors):
    result = []
    for i in range(5):
        value = total[i] if total is not None else None
        for k in range(5):
            term = blocks(i, k) * vectors[k]
            value = term if value is None else value + term
        result.append(value)
    return result


def apply_dense(diag, coupling, columns, own, table, chunks, rows, remap=None):
    image = product(None, lambda i, k: diag[i, k, rows, :], own)
    for n in range(6):
        index = columns[n, rows, :]
        if remap is not None:
            index = remap(index)
        decoded = decode(index, chunks)
        picked = [pick(functools.partial(table, k), decoded, chunks) for k in range(5)]
        image = product(image, lambda i, k: coupling[n, i, k, rows, :], picked)
    return image


def padded(value):
    return jnp.concatenate([value, jnp.zeros((3, value.shape[1]), value.dtype)], axis=0)


def rows_of(parts):
    return jnp.concatenate([jnp.sum(part, axis=0, keepdims=True) for part in parts], axis=0)


def channels(field, group):
    zero = jnp.zeros((3, LANES), F32)
    return jnp.concatenate([field[k, group : group + 1, :] for k in range(5)] + [zero], axis=0)


def split3(value):
    first = value.astype(jnp.bfloat16)
    rest = value - first.astype(F32)
    second = rest.astype(jnp.bfloat16)
    third = (rest - second.astype(F32)).astype(jnp.bfloat16)
    return first, second, third


def restrict(residual, aggregate, number, store):
    groups = number // LANES
    total = jnp.zeros((3 * 8 * groups, LANES), F32)
    step = 4 * LANES
    for start in range(0, residual.shape[1], 4):
        parts = range(start, start + 4)
        index = jnp.concatenate([aggregate[g : g + 1, :] for g in parts], axis=1)
        value = jnp.concatenate([channels(residual, g) for g in parts], axis=1)
        high = index >> 7
        low = index & (LANES - 1)
        left = []
        for piece in split3(value):
            wide = piece.astype(F32)
            left += [jnp.where(high == h, wide, 0.0) for h in range(groups)]
        left = jnp.concatenate(left, axis=0).astype(jnp.bfloat16)
        lanes = lax.broadcasted_iota(jnp.int32, (LANES, step), 0)
        hot = jnp.where(lanes == low, 1.0, 0.0).astype(jnp.bfloat16)
        total = total + lax.dot_general(
            left, hot, (((1,), (1,)), ((), ())), preferred_element_type=F32
        )
    size = 8 * groups
    summed = total[:size] + total[size : 2 * size] + total[2 * size :]
    for h in range(groups):
        store(h, summed[h * 8 : h * 8 + 8])


HALVES = (slice(0, 8), slice(8, 16))


def fine_table(x, received):
    r3, r2, r1, r0 = received
    low, high = r0[...] + r1[...], r2[...] + r3[...]

    def table(k, t):
        if t < 16:
            return x[k, t : t + 1, :]
        return (low, high)[t - 16][k : k + 1]

    return table


def pack_sends(x, where, live, outs):
    decoded = decode(where[...], 16)
    for k in range(5):
        picked = pick(lambda t: x[k, t : t + 1, :], decoded, 16) * live[...]
        for j in range(4):
            outs[j][k : k + 1, :] = picked[j : j + 1, :]


def send_kernel(x, send, count, s0, s1, s2, s3, where, live):
    lane = lax.broadcasted_iota(jnp.int32, (1, LANES), 1)
    for j in range(4):
        first = SLOT_ROWS * ((3 - j) % 2)
        row = send[j : j + 1, :]
        where[j : j + 1, :] = jnp.concatenate([row, row], axis=1)
        inside = (lane >= first) & (lane < first + count[j])
        live[j : j + 1, :] = jnp.where(inside, 1.0, 0.0)
    pack_sends(x, where, live, (s0, s1, s2, s3))


def fine_kernel(last, x, b, diag, inverse, coupling, columns, where, live, r3, r2, r1, r0, *rest):
    if last:
        (new,) = rest
    else:
        s0, s1, s2, s3, new = rest
    table = fine_table(x, (r3, r2, r1, r0))
    for rows in HALVES:
        own = [x[k, rows, :] for k in range(5)]
        image = apply_dense(diag, coupling, columns, own, table, 18, rows)
        left = [b[k, rows, :] - image[k] for k in range(5)]
        change = product(None, lambda i, k: inverse[i, k, rows, :], left)
        for k in range(5):
            new[k, rows, :] = own[k] + RELAX * change[k]
    if not last:
        pack_sends(new, where, live, (s0, s1, s2, s3))


def down_kernel(
    x, b, diag, coupling, columns, aggregate, m_inverse, r3, r2, r1, r0, rhs, e, residual
):
    table = fine_table(x, (r3, r2, r1, r0))
    for rows in HALVES:
        own = [x[k, rows, :] for k in range(5)]
        image = apply_dense(diag, coupling, columns, own, table, 18, rows)
        for k in range(5):
            residual[k, rows, :] = b[k, rows, :] - image[k]

    def store(h, value):
        for k in range(5):
            rhs[k, h : h + 1, :] = value[k : k + 1]

    restrict(residual, aggregate, ROWS_MID, store)
    change = product(None, lambda i, k: m_inverse[i, k], [rhs[k] for k in range(5)])
    for k in range(5):
        e[k] = RELAX * change[k]


def middle_remap(index):
    left = index + (8 * LANES + LANES - RIM_ROWS)
    own = index - RIM_ROWS
    right = index + (9 * LANES - RIM_ROWS - ROWS_MID)
    partner = index - 2 * RIM_ROWS
    return jnp.where(
        index < RIM_ROWS,
        left,
        jnp.where(
            index < RIM_ROWS + ROWS_MID,
            own,
            jnp.where(index < 2 * RIM_ROWS + ROWS_MID, right, partner),
        ),
    )


def middle_image(e, right, left, partner, diag, coupling, columns):
    def table(k, t):
        if t < 4:
            return e[k, t : t + 1, :]
        if t < 8:
            return partner[k, t - 4 : t - 3, :]
        return left[k, 3:4, :] if t == 8 else right[k, 0:1, :]

    own = [e[k] for k in range(5)]
    return own, apply_dense(diag, coupling, columns, own, table, 10, slice(0, 4), middle_remap)


def middle_update(e, rhs, diag, inverse, coupling, columns, right, left, partner):
    own, image = middle_image(e, right, left, partner, diag, coupling, columns)
    gap = [rhs[k] - image[k] for k in range(5)]
    change = product(None, lambda i, k: inverse[i, k], gap)
    return [own[k] + RELAX * change[k] for k in range(5)]


def middle_kernel(e, rhs, diag, inverse, coupling, columns, right, left, partner, new):
    done = middle_update(e, rhs, diag, inverse, coupling, columns, right, left, partner)
    for k in range(5):
        new[k] = done[k]


def coarse_down_kernel(
    e, rhs, diag, coupling, columns, right, left, partner, aggregate, c_inverse, c_rhs, c_new, residual
):
    own, image = middle_image(e, right, left, partner, diag, coupling, columns)
    for k in range(5):
        residual[k] = rhs[k] - image[k]

    def store(h, value):
        c_rhs[...] = value[:5]
        c_new[...] = RELAX * rows_of([c_inverse[i] * value[:5] for i in range(5)])

    restrict(residual, aggregate, ROWS_COARSE, store)


def coarse_rows(field, others, diag, inverse, coupling, columns, rhs):
    own = field[...]
    members = [padded(r[...]) for r in (field,) + others]
    parts = [diag[i] * own for i in range(5)]
    for n in range(6):
        decoded = decode(jnp.broadcast_to(columns[n : n + 1, :], (8, LANES)), 4)
        picked = pick(lambda t: members[t], decoded, 4)[:5]
        for i in range(5):
            parts[i] = parts[i] + coupling[n, i] * picked
    gap = rhs[...] - rows_of(parts)
    return own + RELAX * rows_of([inverse[i] * gap for i in range(5)])


def coarse_kernel(field, rhs, diag, inverse, coupling, columns, p3, p2, p1, new):
    new[...] = coarse_rows(field, (p1, p2, p3), diag, inverse, coupling, columns, rhs)


def coarse_up_kernel(field, rhs, diag, inverse, coupling, columns, p3, p2, p1, e, aggregate, new):
    done = coarse_rows(field, (p1, p2, p3), diag, inverse, coupling, columns, rhs)
    decoded = decode(aggregate[...], 1)
    for k in range(5):
        new[k] = e[k] + pick(lambda t: done[k : k + 1], decoded, 1)


def middle_up_kernel(
    e, rhs, diag, inverse, coupling, columns, right, left, partner, x, aggregate, where, live,
    s0, s1, s2, s3, new
):
    done = middle_update(e, rhs, diag, inverse, coupling, columns, right, left, partner)
    for rows in HALVES:
        decoded = decode(aggregate[rows, :], 4)
        for k in range(5):
            new[k, rows, :] = x[k, rows, :] + pick(lambda t: done[k][t : t + 1], decoded, 4)
    pack_sends(new, where, live, (s0, s1, s2, s3))


VMEM = pl.BlockSpec(memory_space=pltpu.VMEM)
SMEM = pl.BlockSpec(memory_space=pltpu.SMEM)


def call(name, kernel, args, shapes, scratch=(), scalars=()):
    return pl.pallas_call(
        kernel,
        name=name,
        out_shape=[s if isinstance(s, jax.ShapeDtypeStruct) else jax.ShapeDtypeStruct(s, F32) for s in shapes],
        in_specs=[SMEM if i in scalars else VMEM for i in range(len(args))],
        out_specs=[VMEM] * len(shapes),
        scratch_shapes=[pltpu.VMEM(s, F32) for s in scratch],
        compiler_params=pltpu.CompilerParams(vmem_limit_bytes=16 * 1024 * 1024),
    )(*args)


def passed_along(x, by):
    size = lax.axis_size("dom")
    return lax.ppermute(x, "dom", [(i, (i + by) % size) for i in range(size)])


def group_swap(x, mask):
    return lax.ppermute(x, "grp", [(i, i ^ mask) for i in range(lax.axis_size("grp"))])


def per_device(
    right_side, initial_guess, fine_diag, fine_inverse, fine_coupling, fine_columns, fine_send, fine_count,
    fine_aggregate, middle_diag, middle_inverse, middle_coupling, middle_columns, middle_aggregate,
    coarse_diag, coarse_inverse, coarse_coupling, coarse_columns,
):
    def dense(array):
        return array.reshape(array.shape[2:-1] + (array.shape[-1] // LANES, LANES))

    b, x = dense(right_side), dense(initial_guess)
    f_mats = tuple(map(dense, (fine_diag, fine_inverse, fine_coupling, fine_columns)))
    f_send, f_count, f_aggregate = fine_send[0, 0], fine_count[0, 0], dense(fine_aggregate)
    m_mats = tuple(map(dense, (middle_diag, middle_inverse, middle_coupling, middle_columns)))
    m_aggregate = dense(middle_aggregate)
    c_mats = (coarse_diag[0, 0], coarse_inverse[0, 0], coarse_coupling[0, 0], coarse_columns[0, 0])

    slots = [(5, LANES)] * 4
    fine = (5, ROWS_FINE // LANES, LANES)
    mid = (5, ROWS_MID // LANES, LANES)
    coarse = (5, ROWS_COARSE)

    def fine_exchange(sends):
        return [passed_along(sends[3 - j], -OFFSETS[j]) for j in (3, 2, 1, 0)]

    def middle_exchange(e):
        right = passed_along(e, -1)
        left = passed_along(e, 1)
        return [right, left, group_swap(e, 1)]

    def coarse_exchange(c):
        return [group_swap(c, mask) for mask in (3, 2, 1)]

    *sends, where, live = call(
        "send", send_kernel, (x, f_send, f_count),
        slots + [jax.ShapeDtypeStruct((4, LANES), jnp.int32), (4, LANES)], scalars=(2,),
    )

    def fine_sweep(name, x, sends, last=False):
        out = call(
            name,
            functools.partial(fine_kernel, last),
            (x, b) + f_mats + (where, live, *fine_exchange(sends)),
            [fine] if last else slots + [fine],
        )
        return out[-1], out[:-1]

    x, sends = fine_sweep("fine_1", x, sends)
    x, sends = fine_sweep("fine_2", x, sends)
    rhs, e = call(
        "down",
        down_kernel,
        (x, b, f_mats[0], f_mats[2], f_mats[3], f_aggregate, m_mats[1], *fine_exchange(sends)),
        [mid, mid],
        [fine],
    )

    def middle_sweep(name, e):
        return call(name, middle_kernel, (e, rhs) + m_mats + tuple(middle_exchange(e)), [mid])[0]

    e = middle_sweep("middle_2", e)
    c_rhs, c = call(
        "coarse_down",
        coarse_down_kernel,
        (e, rhs, m_mats[0], m_mats[2], m_mats[3], *middle_exchange(e), m_aggregate, c_mats[1]),
        [coarse, coarse],
        [mid],
    )
    (c,) = call("coarse_2", coarse_kernel, (c, c_rhs) + c_mats + tuple(coarse_exchange(c)), [coarse])
    (e,) = call(
        "coarse_3",
        coarse_up_kernel,
        (c, c_rhs) + c_mats + tuple(coarse_exchange(c)) + (e, m_aggregate),
        [mid],
    )
    e = middle_sweep("middle_3", e)
    *sends, x = call(
        "middle_4",
        middle_up_kernel,
        (e, rhs) + m_mats + tuple(middle_exchange(e)) + (x, f_aggregate, where, live),
        slots + [fine],
    )
    x, sends = fine_sweep("fine_4", x, sends)
    x, _ = fine_sweep("fine_5", x, sends, last=True)
    return x.reshape(1, 1, 5, ROWS_FINE)


def solution(mesh):
    def spec(rank):
        return P("grp", "dom", *([None] * (rank - 2)))

    ranks = (4, 4, 5, 5, 6, 4, 4, 3, 3, 5, 5, 6, 4, 3, 5, 5, 6, 4)
    return jax.shard_map(
        per_device,
        mesh=mesh,
        in_specs=tuple(spec(rank) for rank in ranks),
        out_specs=spec(4),
        check_vma=False,
    )
```

```python
import functools

import jax
import jax.numpy as jnp
from jax import lax
from jax.experimental import pallas as pl
from jax.experimental.pallas import tpu as pltpu
from jax.sharding import PartitionSpec as P

ROWS_FINE = 2048
ROWS_MID = 512
ROWS_COARSE = 128
SLOT_ROWS = 64
RIM_ROWS = 32
LANES = 128
OFFSETS = (-2, -1, 1, 2)
RELAX = 0.8
F32 = jnp.float32


def lane_pick(chunk, index):
    return jnp.take_along_axis(chunk, index, axis=1, mode="promise_in_bounds")


def decode(index, chunks):
    low = index & (LANES - 1)
    odd = [(index & (LANES << bit)) != 0 for bit in range((chunks - 1).bit_length())]
    return low, odd


def pick(table, decoded, chunks):
    low, odd = decoded
    level = [lane_pick(jnp.broadcast_to(table(t), low.shape), low) for t in range(chunks)]
    for bit in odd:
        level = [
            jnp.where(bit, level[i + 1], level[i]) if i + 1 < len(level) else level[i]
            for i in range(0, len(level), 2)
        ]
    return level[0]


def product(total, blocks, vectors):
    result = []
    for i in range(5):
        value = total[i] if total is not None else None
        for k in range(5):
            term = blocks(i, k) * vectors[k]
            value = term if value is None else value + term
        result.append(value)
    return result


def apply_dense(diag, coupling, columns, own, table, chunks, rows, remap=None):
    image = product(None, lambda i, k: diag[i, k, rows, :], own)
    for n in range(6):
        index = columns[n, rows, :]
        if remap is not None:
            index = remap(index)
        decoded = decode(index, chunks)
        picked = [pick(functools.partial(table, k), decoded, chunks) for k in range(5)]
        image = product(image, lambda i, k: coupling[n, i, k, rows, :], picked)
    return image


def padded(value):
    return jnp.concatenate([value, jnp.zeros((3, value.shape[1]), value.dtype)], axis=0)


def rows_of(parts):
    return jnp.concatenate([jnp.sum(part, axis=0, keepdims=True) for part in parts], axis=0)


def channels(field, group):
    zero = jnp.zeros((3, LANES), F32)
    return jnp.concatenate([field[k, group : group + 1, :] for k in range(5)] + [zero], axis=0)


def split3(value):
    first = value.astype(jnp.bfloat16)
    rest = value - first.astype(F32)
    second = rest.astype(jnp.bfloat16)
    third = (rest - second.astype(F32)).astype(jnp.bfloat16)
    return first, second, third


def restrict(residual, aggregate, number, store):
    groups = number // LANES
    total = jnp.zeros((3 * 8 * groups, LANES), F32)
    step = 4 * LANES
    for start in range(0, residual.shape[1], 4):
        parts = range(start, start + 4)
        index = jnp.concatenate([aggregate[g : g + 1, :] for g in parts], axis=1)
        value = jnp.concatenate([channels(residual, g) for g in parts], axis=1)
        high = index >> 7
        low = index & (LANES - 1)
        left = []
        for piece in split3(value):
            wide = piece.astype(F32)
            left += [jnp.where(high == h, wide, 0.0) for h in range(groups)]
        left = jnp.concatenate(left, axis=0).astype(jnp.bfloat16)
        lanes = lax.broadcasted_iota(jnp.int32, (LANES, step), 0)
        hot = jnp.where(lanes == low, 1.0, 0.0).astype(jnp.bfloat16)
        total = total + lax.dot_general(
            left, hot, (((1,), (1,)), ((), ())), preferred_element_type=F32
        )
    size = 8 * groups
    summed = total[:size] + total[size : 2 * size] + total[2 * size :]
    for h in range(groups):
        store(h, summed[h * 8 : h * 8 + 8])


HALVES = (slice(0, 8), slice(8, 16))


def fine_table(x, received):
    r3, r2, r1, r0 = received
    low, high = r0[...] + r1[...], r2[...] + r3[...]

    def table(k, t):
        if t < 16:
            return x[k, t : t + 1, :]
        return (low, high)[t - 16][k : k + 1]

    return table


def pack_sends(x, where, live, outs):
    decoded = decode(where[...], 16)
    for k in range(5):
        picked = pick(lambda t: x[k, t : t + 1, :], decoded, 16) * live[...]
        for j in range(4):
            outs[j][k : k + 1, :] = picked[j : j + 1, :]


def send_kernel(
    send_far, count_far, x_far, b_far, diag_far, inverse_far, coupling_far, columns_far,
    s0, s1, s2, s3, where, live, x, b, diag, inverse, coupling, columns, send, count, done
):
    pairs = (
        (send_far, send), (count_far, count), (x_far, x), (columns_far, columns), (b_far, b),
        (diag_far, diag), (inverse_far, inverse), (coupling_far, coupling),
    )
    copies = [pltpu.make_async_copy(a, z, done.at[i]) for i, (a, z) in enumerate(pairs)]
    for copy in copies:
        copy.start()
    for copy in copies[:3]:
        copy.wait()
    lane = lax.broadcasted_iota(jnp.int32, (1, LANES), 1)
    for j in range(4):
        first = SLOT_ROWS * ((3 - j) % 2)
        row = send[j : j + 1, :]
        where[j : j + 1, :] = jnp.concatenate([row, row], axis=1)
        end = jnp.broadcast_to(count[0:1, j : j + 1], (1, LANES)) + first
        live[j : j + 1, :] = jnp.where((lane >= first) & (lane < end), 1.0, 0.0)
    pack_sends(x, where, live, (s0, s1, s2, s3))
    for copy in copies[3:]:
        copy.wait()


def fine_kernel(last, x, b, diag, inverse, coupling, columns, where, live, r3, r2, r1, r0, *rest):
    if last:
        (new,) = rest
    else:
        s0, s1, s2, s3, new = rest
    table = fine_table(x, (r3, r2, r1, r0))
    for rows in HALVES:
        own = [x[k, rows, :] for k in range(5)]
        image = apply_dense(diag, coupling, columns, own, table, 18, rows)
        left = [b[k, rows, :] - image[k] for k in range(5)]
        change = product(None, lambda i, k: inverse[i, k, rows, :], left)
        for k in range(5):
            new[k, rows, :] = own[k] + RELAX * change[k]
    if not last:
        pack_sends(new, where, live, (s0, s1, s2, s3))


def down_kernel(
    x, b, diag, coupling, columns, aggregate, m_inverse, r3, r2, r1, r0, rhs, e, residual
):
    table = fine_table(x, (r3, r2, r1, r0))
    for rows in HALVES:
        own = [x[k, rows, :] for k in range(5)]
        image = apply_dense(diag, coupling, columns, own, table, 18, rows)
        for k in range(5):
            residual[k, rows, :] = b[k, rows, :] - image[k]

    def store(h, value):
        for k in range(5):
            rhs[k, h : h + 1, :] = value[k : k + 1]

    restrict(residual, aggregate, ROWS_MID, store)
    change = product(None, lambda i, k: m_inverse[i, k], [rhs[k] for k in range(5)])
    for k in range(5):
        e[k] = RELAX * change[k]


def middle_remap(index):
    left = index + (8 * LANES + LANES - RIM_ROWS)
    own = index - RIM_ROWS
    right = index + (9 * LANES - RIM_ROWS - ROWS_MID)
    partner = index - 2 * RIM_ROWS
    return jnp.where(
        index < RIM_ROWS,
        left,
        jnp.where(
            index < RIM_ROWS + ROWS_MID,
            own,
            jnp.where(index < 2 * RIM_ROWS + ROWS_MID, right, partner),
        ),
    )


def middle_image(e, right, left, partner, diag, coupling, columns):
    def table(k, t):
        if t < 4:
            return e[k, t : t + 1, :]
        if t < 8:
            return partner[k, t - 4 : t - 3, :]
        return left[k, 3:4, :] if t == 8 else right[k, 0:1, :]

    own = [e[k] for k in range(5)]
    return own, apply_dense(diag, coupling, columns, own, table, 10, slice(0, 4), middle_remap)


def middle_update(e, rhs, diag, inverse, coupling, columns, right, left, partner):
    own, image = middle_image(e, right, left, partner, diag, coupling, columns)
    gap = [rhs[k] - image[k] for k in range(5)]
    change = product(None, lambda i, k: inverse[i, k], gap)
    return [own[k] + RELAX * change[k] for k in range(5)]


def middle_kernel(e, rhs, diag, inverse, coupling, columns, right, left, partner, new):
    done = middle_update(e, rhs, diag, inverse, coupling, columns, right, left, partner)
    for k in range(5):
        new[k] = done[k]


def coarse_down_kernel(
    e, rhs, diag, coupling, columns, right, left, partner, aggregate, c_inverse, c_rhs, c_new, residual
):
    own, image = middle_image(e, right, left, partner, diag, coupling, columns)
    for k in range(5):
        residual[k] = rhs[k] - image[k]

    def store(h, value):
        c_rhs[...] = value[:5]
        c_new[...] = RELAX * rows_of([c_inverse[i] * value[:5] for i in range(5)])

    restrict(residual, aggregate, ROWS_COARSE, store)


def coarse_rows(field, others, diag, inverse, coupling, columns, rhs):
    own = field[...]
    members = [padded(r[...]) for r in (field,) + others]
    parts = [diag[i] * own for i in range(5)]
    for n in range(6):
        decoded = decode(jnp.broadcast_to(columns[n : n + 1, :], (8, LANES)), 4)
        picked = pick(lambda t: members[t], decoded, 4)[:5]
        for i in range(5):
            parts[i] = parts[i] + coupling[n, i] * picked
    gap = rhs[...] - rows_of(parts)
    return own + RELAX * rows_of([inverse[i] * gap for i in range(5)])


def coarse_kernel(field, rhs, diag, inverse, coupling, columns, p3, p2, p1, new):
    new[...] = coarse_rows(field, (p1, p2, p3), diag, inverse, coupling, columns, rhs)


def coarse_up_kernel(field, rhs, diag, inverse, coupling, columns, p3, p2, p1, e, aggregate, new):
    done = coarse_rows(field, (p1, p2, p3), diag, inverse, coupling, columns, rhs)
    decoded = decode(aggregate[...], 1)
    for k in range(5):
        new[k] = e[k] + pick(lambda t: done[k : k + 1], decoded, 1)


def middle_up_kernel(
    e, rhs, diag, inverse, coupling, columns, right, left, partner, x, aggregate, where, live,
    s0, s1, s2, s3, new
):
    done = middle_update(e, rhs, diag, inverse, coupling, columns, right, left, partner)
    for rows in HALVES:
        decoded = decode(aggregate[rows, :], 4)
        for k in range(5):
            new[k, rows, :] = x[k, rows, :] + pick(lambda t: done[k][t : t + 1], decoded, 4)
    pack_sends(new, where, live, (s0, s1, s2, s3))


VMEM = pl.BlockSpec(memory_space=pltpu.VMEM)


def call(name, kernel, args, shapes, scratch=()):
    return pl.pallas_call(
        kernel,
        name=name,
        out_shape=[jax.ShapeDtypeStruct(s, F32) for s in shapes],
        in_specs=[VMEM] * len(args),
        out_specs=[VMEM] * len(shapes),
        scratch_shapes=[pltpu.VMEM(s, F32) for s in scratch],
        compiler_params=pltpu.CompilerParams(vmem_limit_bytes=16 * 1024 * 1024),
    )(*args)


def passed_along(x, by):
    size = lax.axis_size("dom")
    return lax.ppermute(x, "dom", [(i, (i + by) % size) for i in range(size)])


def group_swap(x, mask):
    return lax.ppermute(x, "grp", [(i, i ^ mask) for i in range(lax.axis_size("grp"))])


def per_device(
    right_side, initial_guess, fine_diag, fine_inverse, fine_coupling, fine_columns, fine_send, fine_count,
    fine_aggregate, middle_diag, middle_inverse, middle_coupling, middle_columns, middle_aggregate,
    coarse_diag, coarse_inverse, coarse_coupling, coarse_columns,
):
    def dense(array):
        return array.reshape(array.shape[2:-1] + (array.shape[-1] // LANES, LANES))

    b, x = dense(right_side), dense(initial_guess)
    f_mats = tuple(map(dense, (fine_diag, fine_inverse, fine_coupling, fine_columns)))
    f_send, f_count, f_aggregate = fine_send[0, 0], fine_count[0], dense(fine_aggregate)
    m_mats = tuple(map(dense, (middle_diag, middle_inverse, middle_coupling, middle_columns)))
    m_aggregate = dense(middle_aggregate)
    c_mats = (coarse_diag[0, 0], coarse_inverse[0, 0], coarse_coupling[0, 0], coarse_columns[0, 0])

    slots = [(5, LANES)] * 4
    fine = (5, ROWS_FINE // LANES, LANES)
    mid = (5, ROWS_MID // LANES, LANES)
    coarse = (5, ROWS_COARSE)

    def fine_exchange(sends):
        return [passed_along(sends[3 - j], -OFFSETS[j]) for j in (3, 2, 1, 0)]

    def middle_exchange(e):
        right = passed_along(e, -1)
        left = passed_along(e, 1)
        return [right, left, group_swap(e, 1)]

    def coarse_exchange(c):
        return [group_swap(c, mask) for mask in (3, 2, 1)]

    def shape_of(array):
        return jax.ShapeDtypeStruct(array.shape, array.dtype)

    far = (f_send, f_count, x, b) + f_mats
    out = pl.pallas_call(
        send_kernel,
        name="send",
        out_shape=[jax.ShapeDtypeStruct((5, LANES), F32)] * 4
        + [jax.ShapeDtypeStruct((4, LANES), jnp.int32), jax.ShapeDtypeStruct((4, LANES), F32)]
        + [shape_of(array) for array in far[2:]],
        in_specs=[pl.BlockSpec(memory_space=pltpu.HBM)] * len(far),
        out_specs=[VMEM] * 12,
        scratch_shapes=[
            pltpu.VMEM(f_send.shape, jnp.int32),
            pltpu.VMEM(f_count.shape, jnp.int32),
            pltpu.SemaphoreType.DMA((8,)),
        ],
        compiler_params=pltpu.CompilerParams(vmem_limit_bytes=16 * 1024 * 1024),
    )(*(pltpu.with_memory_space_constraint(array, pltpu.HBM) for array in far))
    sends, (where, live, x, b), f_mats = out[:4], out[4:8], tuple(out[8:])

    def fine_sweep(name, x, sends, last=False):
        out = call(
            name,
            functools.partial(fine_kernel, last),
            (x, b) + f_mats + (where, live, *fine_exchange(sends)),
            [fine] if last else slots + [fine],
        )
        return out[-1], out[:-1]

    x, sends = fine_sweep("fine_1", x, sends)
    x, sends = fine_sweep("fine_2", x, sends)
    rhs, e = call(
        "down",
        down_kernel,
        (x, b, f_mats[0], f_mats[2], f_mats[3], f_aggregate, m_mats[1], *fine_exchange(sends)),
        [mid, mid],
        [fine],
    )

    def middle_sweep(name, e):
        return call(name, middle_kernel, (e, rhs) + m_mats + tuple(middle_exchange(e)), [mid])[0]

    e = middle_sweep("middle_2", e)
    c_rhs, c = call(
        "coarse_down",
        coarse_down_kernel,
        (e, rhs, m_mats[0], m_mats[2], m_mats[3], *middle_exchange(e), m_aggregate, c_mats[1]),
        [coarse, coarse],
        [mid],
    )
    (c,) = call("coarse_2", coarse_kernel, (c, c_rhs) + c_mats + tuple(coarse_exchange(c)), [coarse])
    (e,) = call(
        "coarse_3",
        coarse_up_kernel,
        (c, c_rhs) + c_mats + tuple(coarse_exchange(c)) + (e, m_aggregate),
        [mid],
    )
    e = middle_sweep("middle_3", e)
    *sends, x = call(
        "middle_4",
        middle_up_kernel,
        (e, rhs) + m_mats + tuple(middle_exchange(e)) + (x, f_aggregate, where, live),
        slots + [fine],
    )
    x, sends = fine_sweep("fine_4", x, sends)
    x, _ = fine_sweep("fine_5", x, sends, last=True)
    return x.reshape(1, 1, 5, ROWS_FINE)


def solution(mesh):
    def spec(rank):
        return P("grp", "dom", *([None] * (rank - 2)))

    ranks = (4, 4, 5, 5, 6, 4, 4, 3, 3, 5, 5, 6, 4, 3, 5, 5, 6, 4)
    return jax.shard_map(
        per_device,
        mesh=mesh,
        in_specs=tuple(spec(rank) for rank in ranks),
        out_specs=spec(4),
        check_vma=False,
    )
```

```python
import functools

import jax
import jax.numpy as jnp
from jax import lax
from jax.experimental import pallas as pl
from jax.experimental.pallas import tpu as pltpu
from jax.sharding import PartitionSpec as P

ROWS_FINE = 2048
ROWS_MID = 512
ROWS_COARSE = 128
SLOT_ROWS = 64
RIM_ROWS = 32
LANES = 128
OFFSETS = (-2, -1, 1, 2)
RELAX = 0.8
F32 = jnp.float32


def lane_pick(chunk, index):
    return jnp.take_along_axis(chunk, index, axis=1, mode="promise_in_bounds")


def decode(index, chunks):
    low = index & (LANES - 1)
    odd = [(index & (LANES << bit)) != 0 for bit in range((chunks - 1).bit_length())]
    return low, odd


def pick(table, decoded, chunks):
    low, odd = decoded
    level = [lane_pick(jnp.broadcast_to(table(t), low.shape), low) for t in range(chunks)]
    for bit in odd:
        level = [
            jnp.where(bit, level[i + 1], level[i]) if i + 1 < len(level) else level[i]
            for i in range(0, len(level), 2)
        ]
    return level[0]


def product(total, blocks, vectors):
    result = []
    for i in range(5):
        value = total[i] if total is not None else None
        for k in range(5):
            term = blocks(i, k) * vectors[k]
            value = term if value is None else value + term
        result.append(value)
    return result


def apply_dense(diag, coupling, columns, own, table, chunks, rows, remap=None):
    image = product(None, lambda i, k: diag[i, k, rows, :], own)
    for n in range(6):
        index = columns[n, rows, :]
        if remap is not None:
            index = remap(index)
        decoded = decode(index, chunks)
        picked = [pick(functools.partial(table, k), decoded, chunks) for k in range(5)]
        image = product(image, lambda i, k: coupling[n, i, k, rows, :], picked)
    return image


def padded(value):
    return jnp.concatenate([value, jnp.zeros((3, value.shape[1]), value.dtype)], axis=0)


def rows_of(parts):
    return jnp.concatenate([jnp.sum(part, axis=0, keepdims=True) for part in parts], axis=0)


def channels(field, group):
    zero = jnp.zeros((3, LANES), F32)
    return jnp.concatenate([field[k, group : group + 1, :] for k in range(5)] + [zero], axis=0)


def split3(value):
    first = value.astype(jnp.bfloat16)
    rest = value - first.astype(F32)
    second = rest.astype(jnp.bfloat16)
    third = (rest - second.astype(F32)).astype(jnp.bfloat16)
    return first, second, third


def restrict(residual, aggregate, number, store):
    groups = number // LANES
    total = jnp.zeros((3 * 8 * groups, LANES), F32)
    step = 4 * LANES
    for start in range(0, residual.shape[1], 4):
        parts = range(start, start + 4)
        index = jnp.concatenate([aggregate[g : g + 1, :] for g in parts], axis=1)
        value = jnp.concatenate([channels(residual, g) for g in parts], axis=1)
        high = index >> 7
        low = index & (LANES - 1)
        left = []
        for piece in split3(value):
            wide = piece.astype(F32)
            left += [jnp.where(high == h, wide, 0.0) for h in range(groups)]
        left = jnp.concatenate(left, axis=0).astype(jnp.bfloat16)
        lanes = lax.broadcasted_iota(jnp.int32, (LANES, step), 0)
        hot = jnp.where(lanes == low, 1.0, 0.0).astype(jnp.bfloat16)
        total = total + lax.dot_general(
            left, hot, (((1,), (1,)), ((), ())), preferred_element_type=F32
        )
    size = 8 * groups
    summed = total[:size] + total[size : 2 * size] + total[2 * size :]
    for h in range(groups):
        store(h, summed[h * 8 : h * 8 + 8])


HALVES = (slice(0, 8), slice(8, 16))


def fine_table(x, received):
    r3, r2, r1, r0 = received
    low, high = r0[...] + r1[...], r2[...] + r3[...]

    def table(k, t):
        if t < 16:
            return x[k, t : t + 1, :]
        return (low, high)[t - 16][k : k + 1]

    return table


def pack_sends(x, where, live, outs):
    decoded = decode(where[...], 16)
    for k in range(5):
        picked = pick(lambda t: x[k, t : t + 1, :], decoded, 16) * live[...]
        for j in range(4):
            outs[j][k : k + 1, :] = picked[j : j + 1, :]


def send_kernel(
    send_far, count_far, x_far, b_far, diag_far, inverse_far, coupling_far, columns_far,
    s0, s1, s2, s3, where, live, x, b, diag, inverse, coupling, columns, send, count, done
):
    pairs = (
        (send_far, send), (count_far, count), (x_far, x), (columns_far, columns), (b_far, b),
        (diag_far, diag), (inverse_far, inverse), (coupling_far, coupling),
    )
    copies = [pltpu.make_async_copy(a, z, done.at[i]) for i, (a, z) in enumerate(pairs)]
    for copy in copies:
        copy.start()
    for copy in copies[:3]:
        copy.wait()
    lane = lax.broadcasted_iota(jnp.int32, (1, LANES), 1)
    for j in range(4):
        first = SLOT_ROWS * ((3 - j) % 2)
        row = send[j : j + 1, :]
        where[j : j + 1, :] = jnp.concatenate([row, row], axis=1)
        end = jnp.broadcast_to(count[0:1, j : j + 1], (1, LANES)) + first
        live[j : j + 1, :] = jnp.where((lane >= first) & (lane < end), 1.0, 0.0)
    pack_sends(x, where, live, (s0, s1, s2, s3))
    for copy in copies[3:]:
        copy.wait()


def fine_kernel(last, x, b, diag, inverse, coupling, columns, where, live, r3, r2, r1, r0, *rest):
    if last:
        (new,) = rest
    else:
        s0, s1, s2, s3, new = rest
    table = fine_table(x, (r3, r2, r1, r0))
    for rows in HALVES:
        own = [x[k, rows, :] for k in range(5)]
        image = apply_dense(diag, coupling, columns, own, table, 18, rows)
        left = [b[k, rows, :] - image[k] for k in range(5)]
        change = product(None, lambda i, k: inverse[i, k, rows, :], left)
        for k in range(5):
            new[k, rows, :] = own[k] + RELAX * change[k]
    if not last:
        pack_sends(new, where, live, (s0, s1, s2, s3))


def down_kernel(
    x, b, diag, coupling, columns, aggregate, m_inverse, r1, r0, r3, r2, rhs, e, residual
):
    table = fine_table(x, (r3, r2, r1, r0))
    for rows in HALVES:
        own = [x[k, rows, :] for k in range(5)]
        image = apply_dense(diag, coupling, columns, own, table, 18, rows)
        for k in range(5):
            residual[k, rows, :] = b[k, rows, :] - image[k]

    def store(h, value):
        for k in range(5):
            rhs[k, h : h + 1, :] = value[k : k + 1]

    restrict(residual, aggregate, ROWS_MID, store)
    change = product(None, lambda i, k: m_inverse[i, k], [rhs[k] for k in range(5)])
    for k in range(5):
        e[k] = RELAX * change[k]


def middle_remap(index):
    left = index + (8 * LANES + LANES - RIM_ROWS)
    own = index - RIM_ROWS
    right = index + (9 * LANES - RIM_ROWS - ROWS_MID)
    partner = index - 2 * RIM_ROWS
    return jnp.where(
        index < RIM_ROWS,
        left,
        jnp.where(
            index < RIM_ROWS + ROWS_MID,
            own,
            jnp.where(index < 2 * RIM_ROWS + ROWS_MID, right, partner),
        ),
    )


def middle_image(e, right, left, partner, diag, coupling, columns):
    def table(k, t):
        if t < 4:
            return e[k, t : t + 1, :]
        if t < 8:
            return partner[k, t - 4 : t - 3, :]
        return left[k, 3:4, :] if t == 8 else right[k, 0:1, :]

    own = [e[k] for k in range(5)]
    return own, apply_dense(diag, coupling, columns, own, table, 10, slice(0, 4), middle_remap)


def middle_update(e, rhs, diag, inverse, coupling, columns, right, left, partner):
    own, image = middle_image(e, right, left, partner, diag, coupling, columns)
    gap = [rhs[k] - image[k] for k in range(5)]
    change = product(None, lambda i, k: inverse[i, k], gap)
    return [own[k] + RELAX * change[k] for k in range(5)]


def middle_kernel(e, rhs, diag, inverse, coupling, columns, right, left, partner, new):
    done = middle_update(e, rhs, diag, inverse, coupling, columns, right, left, partner)
    for k in range(5):
        new[k] = done[k]


def coarse_down_kernel(
    e, rhs, diag, coupling, columns, right, left, partner, aggregate, c_inverse, c_rhs, c_new, residual
):
    own, image = middle_image(e, right, left, partner, diag, coupling, columns)
    for k in range(5):
        residual[k] = rhs[k] - image[k]

    def store(h, value):
        c_rhs[...] = value[:5]
        c_new[...] = RELAX * rows_of([c_inverse[i] * value[:5] for i in range(5)])

    restrict(residual, aggregate, ROWS_COARSE, store)


def coarse_rows(field, others, diag, inverse, coupling, columns, rhs):
    own = field[...]
    members = [padded(r[...]) for r in (field,) + others]
    parts = [diag[i] * own for i in range(5)]
    for n in range(6):
        decoded = decode(jnp.broadcast_to(columns[n : n + 1, :], (8, LANES)), 4)
        picked = pick(lambda t: members[t], decoded, 4)[:5]
        for i in range(5):
            parts[i] = parts[i] + coupling[n, i] * picked
    gap = rhs[...] - rows_of(parts)
    return own + RELAX * rows_of([inverse[i] * gap for i in range(5)])


def coarse_kernel(field, rhs, diag, inverse, coupling, columns, p3, p2, p1, new):
    new[...] = coarse_rows(field, (p1, p2, p3), diag, inverse, coupling, columns, rhs)


def coarse_up_kernel(field, rhs, diag, inverse, coupling, columns, p3, p2, p1, e, aggregate, new):
    done = coarse_rows(field, (p1, p2, p3), diag, inverse, coupling, columns, rhs)
    decoded = decode(aggregate[...], 1)
    for k in range(5):
        new[k] = e[k] + pick(lambda t: done[k : k + 1], decoded, 1)


def middle_up_kernel(
    e, rhs, diag, inverse, coupling, columns, right, left, partner, x, aggregate, where, live,
    s0, s1, s2, s3, new
):
    done = middle_update(e, rhs, diag, inverse, coupling, columns, right, left, partner)
    for rows in HALVES:
        decoded = decode(aggregate[rows, :], 4)
        for k in range(5):
            new[k, rows, :] = x[k, rows, :] + pick(lambda t: done[k][t : t + 1], decoded, 4)
    pack_sends(new, where, live, (s0, s1, s2, s3))


VMEM = pl.BlockSpec(memory_space=pltpu.VMEM)


def call(name, kernel, args, shapes, scratch=()):
    return pl.pallas_call(
        kernel,
        name=name,
        out_shape=[jax.ShapeDtypeStruct(s, F32) for s in shapes],
        in_specs=[VMEM] * len(args),
        out_specs=[VMEM] * len(shapes),
        scratch_shapes=[pltpu.VMEM(s, F32) for s in scratch],
        compiler_params=pltpu.CompilerParams(vmem_limit_bytes=16 * 1024 * 1024),
    )(*args)


def passed_along(x, by):
    size = lax.axis_size("dom")
    return lax.ppermute(x, "dom", [(i, (i + by) % size) for i in range(size)])


def group_swap(x, mask):
    return lax.ppermute(x, "grp", [(i, i ^ mask) for i in range(lax.axis_size("grp"))])


def per_device(
    right_side, initial_guess, fine_diag, fine_inverse, fine_coupling, fine_columns, fine_send, fine_count,
    fine_aggregate, middle_diag, middle_inverse, middle_coupling, middle_columns, middle_aggregate,
    coarse_diag, coarse_inverse, coarse_coupling, coarse_columns,
):
    def dense(array):
        return array.reshape(array.shape[2:-1] + (array.shape[-1] // LANES, LANES))

    b, x = dense(right_side), dense(initial_guess)
    f_mats = tuple(map(dense, (fine_diag, fine_inverse, fine_coupling, fine_columns)))
    f_send, f_count, f_aggregate = fine_send[0, 0], fine_count[0], dense(fine_aggregate)
    m_mats = tuple(map(dense, (middle_diag, middle_inverse, middle_coupling, middle_columns)))
    m_aggregate = dense(middle_aggregate)
    c_mats = (coarse_diag[0, 0], coarse_inverse[0, 0], coarse_coupling[0, 0], coarse_columns[0, 0])

    slots = [(5, LANES)] * 4
    fine = (5, ROWS_FINE // LANES, LANES)
    mid = (5, ROWS_MID // LANES, LANES)
    coarse = (5, ROWS_COARSE)

    def fine_exchange(sends, blocks=(3, 2, 1, 0)):
        return [passed_along(sends[3 - j], -OFFSETS[j]) for j in blocks]

    def middle_exchange(e):
        right = passed_along(e, -1)
        left = passed_along(e, 1)
        return [right, left, group_swap(e, 1)]

    def coarse_exchange(c):
        return [group_swap(c, mask) for mask in (3, 2, 1)]

    def shape_of(array):
        return jax.ShapeDtypeStruct(array.shape, array.dtype)

    far = (f_send, f_count, x, b) + f_mats
    out = pl.pallas_call(
        send_kernel,
        name="send",
        out_shape=[jax.ShapeDtypeStruct((5, LANES), F32)] * 4
        + [jax.ShapeDtypeStruct((4, LANES), jnp.int32), jax.ShapeDtypeStruct((4, LANES), F32)]
        + [shape_of(array) for array in far[2:]],
        in_specs=[pl.BlockSpec(memory_space=pltpu.HBM)] * len(far),
        out_specs=[VMEM] * 12,
        scratch_shapes=[
            pltpu.VMEM(f_send.shape, jnp.int32),
            pltpu.VMEM(f_count.shape, jnp.int32),
            pltpu.SemaphoreType.DMA((8,)),
        ],
        compiler_params=pltpu.CompilerParams(vmem_limit_bytes=16 * 1024 * 1024),
    )(*(pltpu.with_memory_space_constraint(array, pltpu.HBM) for array in far))
    sends, (where, live, x, b), f_mats = out[:4], out[4:8], tuple(out[8:])

    def fine_sweep(name, x, sends, last=False):
        out = call(
            name,
            functools.partial(fine_kernel, last),
            (x, b) + f_mats + (where, live, *fine_exchange(sends)),
            [fine] if last else slots + [fine],
        )
        return out[-1], out[:-1]

    x, sends = fine_sweep("fine_1", x, sends)
    x, sends = fine_sweep("fine_2", x, sends)
    rhs, e = call(
        "down",
        down_kernel,
        (x, b, f_mats[0], f_mats[2], f_mats[3], f_aggregate, m_mats[1], *fine_exchange(sends, (1, 0, 3, 2))),
        [mid, mid],
        [fine],
    )

    def middle_sweep(name, e):
        return call(name, middle_kernel, (e, rhs) + m_mats + tuple(middle_exchange(e)), [mid])[0]

    e = middle_sweep("middle_2", e)
    c_rhs, c = call(
        "coarse_down",
        coarse_down_kernel,
        (e, rhs, m_mats[0], m_mats[2], m_mats[3], *middle_exchange(e), m_aggregate, c_mats[1]),
        [coarse, coarse],
        [mid],
    )
    (c,) = call("coarse_2", coarse_kernel, (c, c_rhs) + c_mats + tuple(coarse_exchange(c)), [coarse])
    (e,) = call(
        "coarse_3",
        coarse_up_kernel,
        (c, c_rhs) + c_mats + tuple(coarse_exchange(c)) + (e, m_aggregate),
        [mid],
    )
    e = middle_sweep("middle_3", e)
    *sends, x = call(
        "middle_4",
        middle_up_kernel,
        (e, rhs) + m_mats + tuple(middle_exchange(e)) + (x, f_aggregate, where, live),
        slots + [fine],
    )
    x, sends = fine_sweep("fine_4", x, sends)
    x, _ = fine_sweep("fine_5", x, sends, last=True)
    return x.reshape(1, 1, 5, ROWS_FINE)


def solution(mesh):
    def spec(rank):
        return P("grp", "dom", *([None] * (rank - 2)))

    ranks = (4, 4, 5, 5, 6, 4, 4, 3, 3, 5, 5, 6, 4, 3, 5, 5, 6, 4)
    return jax.shard_map(
        per_device,
        mesh=mesh,
        in_specs=tuple(spec(rank) for rank in ranks),
        out_specs=spec(4),
        check_vma=False,
    )
```
